256 devices in a mesh: cache: 64 (over z, y, x_hi), tensor: 4 (over x_lo, core).
Axes of the slice: x: 4 (x_hi: 2, x_lo: 2; x = x_hi * 2 + x_lo), y: 4, z: 8, core: 2. Of those that a mesh axis runs over, the one named last changes fastest.
Arguments:
- candidates: bfloat16 [65536, 1024], P('cache', 'tensor'), may hold values from -6 to 6
- candidate_user: int32 [65536, 1], P('cache'), may hold values from 0 to 127; in each aligned block of 1024 rows (0 to 1023, 1024 to 2047, ...) at most 16 rows name the same one
- history_lengths: int32 [128], P('cache'), may hold values from 1 to 1536, 98304 in all
- w_in: bfloat16 [2, 1024, 4, 1024], P(None, None, None, 'tensor'), may hold values from -0.1875 to 0.1875
- w_out: bfloat16 [2, 1024, 1024], P(None, 'tensor'), may hold values from -0.1875 to 0.1875
- hist_keys: bfloat16 [2, 128, 1536, 1024], P(None, 'cache', None, 'tensor'), may hold values from -6 to 6
- hist_values: bfloat16 [2, 128, 1536, 1024], P(None, 'cache', None, 'tensor'), may hold values from -6 to 6
Outputs:
- scored: bfloat16 [65536, 1024], P('cache', 'tensor')
The draws below stay inside these ranges and needn't reach their ends.
Inputs may be any that keep to these rules, and one draw needn't show every extreme that they name: `candidate_user`: among the 1024 candidates of one index of cache no user is named more than 16 times, a bound that some block reaches. `history_lengths`: some user has exactly 1536 history items.
All inputs are finite; a program needn't handle non-finite values. No bound on the sum of `history_lengths` on one device may be relied on, other than what follows from the above.
Results may differ from the reference program's by a relative error of at most 0.023.
Values may be sent and summed in bfloat16 or wider, within the bound.
No kernel may reach another device: no remote copies, remote signals or barrier semaphores. Data moves between devices by JAX's collectives and lax.ppermute only.
A program may use at most 128 MiB of HBM per device.

```python
import math
import jax
import jax.numpy as jnp
import numpy as np
from jax import lax

D = 1024
HEADS = 8
DH = 128
HD = 1024
LAYERS = 2
HIST = 1536
CAND_DEV = 1024
USERS = 128
CANDS = 65536
MOST = 16
N_CACHE = 64
N_TENSOR = 4


def levels(key, extent, split, low, largest):
    gain, own = 1.0, jax.random.fold_in(key, 6)
    for position, parts in split:
        steps = jnp.exp(jax.random.uniform(jax.random.fold_in(own, position), (parts,), jnp.float32, low / len(split), largest / len(split)))
        gain = gain * jnp.repeat(steps, extent[position] // parts).reshape([-1 if axis == position else 1 for axis in range(len(extent))])
    return gain


def profile(number_of, total, most, slope):
    portions = [(1 << 20) // math.isqrt(standing ** slope) + 1 for standing in range(2, number_of + 1)]
    spare, given = total - most - (number_of - 1), [1] * (number_of - 1)
    while spare > 0:
        movable = [i for i in range(number_of - 1) if given[i] < most]
        whole, remaining = sum([portions[i] for i in movable]), spare
        for i in movable:
            addition = min(most - given[i], max(1, remaining * portions[i] // whole), spare)
            given[i] = given[i] + addition
            spare = spare - addition
    return np.array([most] + given)


def uneven_parts(key, number_of, total, most, skew):
    if number_of == 2:
        one = jax.random.randint(key, (), max(1, total - most), min(most, total - 1) + 1)
        return jnp.stack([one, total - one])
    sizes = jnp.asarray(profile(number_of, total, most, skew), jnp.int32)
    pairs = (number_of - 1) // 2
    donor, receiver = sizes[1:1 + 2 * pairs:2], sizes[2:2 + 2 * pairs:2]
    slack = jnp.minimum(donor - 1, most - receiver)
    passed = jax.random.randint(jax.random.fold_in(key, 1), (pairs,), 0, 1 << 20) % (slack + 1)
    sizes = sizes.at[1:1 + 2 * pairs:2].set(donor - passed).at[2:2 + 2 * pairs:2].set(receiver + passed)
    return sizes[jax.random.permutation(jax.random.fold_in(key, 2), number_of)]


def shared_out(key, own, number, rows, number_of, top, most, skew):
    order = jax.random.permutation(key, number_of)
    crowded, usual = shares(number_of, rows * top, most, skew, True), shares(number_of, rows * top, most, skew, False)
    places = jnp.arange(number_of)

    def named(tallies, turn):
        used = int((tallies > 0).sum())
        fixed = max(1, used // 4)
        passed = fixed + (places - fixed + turn * (used - fixed)) % max(1, number_of - fixed)
        return jnp.zeros((number_of,), jnp.int32).at[order[jnp.where(places < fixed, places, passed)]].set(jnp.asarray(tallies, jnp.int32))

    tallies = jnp.where(number % 4 == 0, named(crowded, number // 4), named(usual, number - number // 4 - 1))
    mixed = jax.random.permutation(jax.random.fold_in(own, 3), number_of)
    donor, sink = mixed[0:number_of // 2 * 2:2], mixed[1:number_of // 2 * 2:2]
    slack = jnp.minimum(tallies[donor] - 1, most - tallies[sink]) // 2
    slack = jnp.where((donor == order[0]) | (sink == order[0]) | (tallies[sink] == 0), 0, jnp.maximum(slack, 0))
    passed = jax.random.randint(jax.random.fold_in(own, 4), (number_of // 2,), 0, 1 << 20) % (slack + 1)
    tallies = tallies.at[donor].add(-passed).at[sink].add(passed)
    items = jnp.searchsorted(jnp.cumsum(tallies), jnp.arange(rows * top), side="right").astype(jnp.int32)
    grid = items.reshape(top, rows).T
    grid = grid[jax.random.permutation(jax.random.fold_in(own, 1), rows)]
    turn = jax.random.randint(jax.random.fold_in(own, 2), (rows, 1), 0, top)
    return jnp.take_along_axis(grid, (jnp.arange(top)[None, :] + turn) % top, axis=1)


def shares(amount, total, limit, slope, full):
    weights = [(1 << 20) // math.isqrt(grade ** slope) + 1 for grade in range(1, amount + 1)]
    largest = limit if full else min(limit, max(-(-total // amount), total * weights[0] // sum(weights)))
    least = 1 if total - largest >= amount - 1 else 0
    counts, rest = [largest] + [least] * (amount - 1), total - largest - least * (amount - 1)
    while rest > 0:
        movable = [i for i in range(1, amount) if counts[i] < largest] or [i for i in range(1, amount) if counts[i] < limit]
        whole, budget = sum([weights[i] for i in movable]), rest
        for i in movable:
            extra = min(limit - counts[i], max(1, budget * weights[i] // whole), rest)
            counts[i] = counts[i] + extra
            rest = rest - extra
    return np.array(counts)


def scatter_about(key, extent, scale, most, cuts=(), dtype=jnp.bfloat16):
    values = jax.random.normal(key, extent, jnp.float32) * scale
    if len(cuts) > 0:
        values = levels(key, extent, cuts, -0.22, 0.18) * values
    return jnp.clip(values, min=-most, max=most).astype(dtype)


def setup_inputs(seed: int = 0) -> dict:
    arg_keys = jax.random.split(jax.random.key(seed), 8)
    candidates = scatter_about(arg_keys[0], (CANDS, D), 1.0, 6.0, ((0, 64), (1, 4)))
    candidate_user_keys = jax.random.split(jax.random.fold_in(arg_keys[1], 1), CANDS // CAND_DEV)
    candidate_user_turns = jax.random.permutation(jax.random.fold_in(arg_keys[1], 3), CANDS // CAND_DEV)
    candidate_user = jax.vmap(lambda own, number: shared_out(jax.random.fold_in(arg_keys[1], 2), own, number, CAND_DEV, USERS, 1, MOST, 2))(candidate_user_keys, candidate_user_turns).reshape((CANDS, 1))
    history_lengths = uneven_parts(arg_keys[2], USERS, USERS * HIST // 2, HIST, 2).astype(jnp.int32)
    w_in = scatter_about(arg_keys[3], (LAYERS, D, 4, HD), D ** -0.5, 0.1875, ((3, 4),))
    w_out = scatter_about(arg_keys[4], (LAYERS, HD, D), HD ** -0.5, 0.1875, ((1, 4),))
    hist_keys = scatter_about(arg_keys[5], (LAYERS, USERS, HIST, HD), 1.0, 6.0, ((1, 64), (3, 4)))
    hist_values = scatter_about(arg_keys[6], (LAYERS, USERS, HIST, HD), 1.0, 6.0, ((1, 64), (3, 4)))
    return {"candidates": candidates, "candidate_user": candidate_user, "history_lengths": history_lengths, "w_in": w_in, "w_out": w_out, "hist_keys": hist_keys, "hist_values": hist_values}


epsilon = 1e-05

def layer_norm(matrix, width):
    row_total = lax.optimization_barrier(jnp.sum(matrix, axis=1))
    squares = lax.optimization_barrier(jnp.sum(matrix * matrix, axis=1))
    center = row_total / width
    spread = squares / width - center * center
    return (matrix - center[:, None]) * lax.rsqrt(spread + epsilon)[:, None]

def rank_block(block_users):
    count = block_users.shape[0]
    same_user = block_users[:, None] == block_users[None, :]
    earlier = jnp.arange(count)[None, :] < jnp.arange(count)[:, None]
    return lax.optimization_barrier(jnp.sum(jnp.logical_and(same_user, earlier), axis=1)).astype(jnp.int32)

def attend_user(operands):
    packed, keys_hist, values_hist, live_mask = operands
    count = packed.shape[0]
    score_scale = DH ** (-0.5)
    queries = packed[:, 0].astype(jnp.float32).reshape(count, HEADS, DH)
    keys_own = packed[:, 1].astype(jnp.float32).reshape(count, HEADS, DH)
    values_own = packed[:, 2].astype(jnp.float32).reshape(count, HEADS, DH)
    keys_all = keys_hist.astype(jnp.float32).reshape(HIST, HEADS, DH)
    values_all = values_hist.astype(jnp.float32).reshape(HIST, HEADS, DH)
    scores = jnp.einsum('phd,jhd->phj', queries, keys_all) * score_scale
    weights = (jax.nn.silu(scores) * live_mask[None, None, :]).astype(jnp.bfloat16)
    history_part = jnp.einsum('phj,jhd->phd', weights.astype(jnp.float32), values_all)
    own_score = lax.optimization_barrier(jnp.sum(queries * keys_own, axis=2)) * score_scale
    own_part = jax.nn.silu(own_score)[:, :, None] * values_own
    return (history_part + own_part).reshape(count, HD).astype(jnp.bfloat16)

def reference(candidates, candidate_user, history_lengths, w_in, w_out, hist_keys, hist_values):
    owner_user = candidate_user[:, 0].astype(jnp.int32)
    rank_index = lax.map(rank_block, owner_user.reshape(N_CACHE, CAND_DEV)).reshape(CANDS)
    source_block = (jnp.arange(CANDS) // CAND_DEV).astype(jnp.int32)
    per_user = N_CACHE * MOST
    slot_index = owner_user * per_user + source_block * MOST + rank_index
    live_mask = (jnp.arange(HIST)[None, :] < history_lengths[:, None]).astype(jnp.float32)
    width_part = HD // N_TENSOR
    hidden_state = candidates
    for layer_index in range(LAYERS):
        state_float = hidden_state.astype(jnp.float32)
        normed = layer_norm(state_float, D).astype(jnp.bfloat16)
        projected = jax.nn.silu(jnp.dot(normed, w_in[layer_index].reshape(D, 4 * HD), preferred_element_type=jnp.float32))
        pieces = projected.reshape(CANDS, 4, HD).astype(jnp.bfloat16)
        packed = jnp.stack([pieces[:, 2], pieces[:, 3], pieces[:, 1]], axis=1)
        buffer = jnp.zeros((USERS * per_user, 3, HD), jnp.bfloat16).at[slot_index].set(packed)
        buffer = buffer.reshape(USERS, per_user, 3, HD)
        attended = lax.map(attend_user, (buffer, hist_keys[layer_index], hist_values[layer_index], live_mask))
        attention = attended.reshape(USERS * per_user, HD)[slot_index]
        gated = (layer_norm(attention.astype(jnp.float32), HD) * pieces[:, 0].astype(jnp.float32)).astype(jnp.bfloat16)
        update = jnp.zeros((CANDS, D), jnp.float32)
        for group_index in range(N_TENSOR):
            lower = group_index * width_part
            term = jnp.dot(gated[:, lower:lower + width_part], w_out[layer_index][lower:lower + width_part], preferred_element_type=jnp.float32).astype(jnp.bfloat16)
            update = update + lax.optimization_barrier(term).astype(jnp.float32)
        hidden_state = (state_float + update).astype(jnp.bfloat16)
    return hidden_state
```

```python
import functools

import jax
import jax.numpy as jnp
from jax import lax
from jax.experimental import pallas as pl
from jax.experimental.pallas import tpu as pltpu
from jax.sharding import PartitionSpec as P

DH = 128
EPS = 1e-05
BF = jnp.bfloat16
F32 = jnp.float32


def silu(x):
    half = 0.5 * x
    return half * jnp.tanh(half) + half


def attend_kernel(len_ref, x_ref, k_ref, v_ref, o_ref, vm_ref):
    users, hist, width = vm_ref.shape
    rows = x_ref.shape[0]
    per_user = rows // users
    slots = 8
    blocks = rows // 256
    each = 256 // users

    @pl.when(pl.program_id(0) == 0)
    def _():
        for u in range(users):
            live = lax.broadcasted_iota(jnp.int32, (hist, width), 0) < len_ref[u]
            vm_ref[u] = jnp.where(live, v_ref[u], jnp.zeros((), BF))

    out_row = lax.broadcasted_iota(jnp.int32, (256, 256), 0)
    in_row = lax.broadcasted_iota(jnp.int32, (256, 256), 1)
    half = slots // users
    target = (
        (in_row % slots) // half * each + in_row // slots * half + in_row % half
    )
    sort = (target == out_row).astype(BF)
    back_target = (
        (out_row % slots) // half * each + out_row // slots * half + out_row % half
    )
    unsort = (back_target == in_row).astype(BF)

    sorted_blocks = [
        jnp.dot(sort, x_ref[b * 256 : (b + 1) * 256, :], preferred_element_type=F32).astype(BF)
        for b in range(blocks)
    ]
    results = []
    scale = 0.5 * DH ** (-0.5)
    for u in range(users):
        q = jnp.concatenate([s[u * each : (u + 1) * each] for s in sorted_blocks], axis=0)
        parts = []
        for h in range(width // DH):
            cols = slice(h * DH, (h + 1) * DH)
            acc = jnp.zeros((per_user, DH), F32)
            for j in range(0, hist, 512):
                s = lax.dot_general(
                    q[:, cols],
                    k_ref[u, j : j + 512, cols],
                    (((1,), (1,)), ((), ())),
                    preferred_element_type=F32,
                )
                s = s * scale
                w = (s * jnp.tanh(s) + s).astype(BF)
                acc = acc + jnp.dot(w, vm_ref[u, j : j + 512, cols], preferred_element_type=F32)
            parts.append(acc.astype(BF))
        results.append(jnp.concatenate(parts, axis=1))
    for b in range(blocks):
        stacked = jnp.concatenate([r[b * each : (b + 1) * each] for r in results], axis=0)
        o_ref[b * 256 : (b + 1) * 256, :] = jnp.dot(
            unsort, stacked, preferred_element_type=F32
        ).astype(BF)


def attend(layer, lengths, x, keys, values, block=512):
    rows, width = x.shape
    users, hist = keys.shape[1:3]
    return pl.pallas_call(
        attend_kernel,
        out_shape=jax.ShapeDtypeStruct((rows, width), BF),
        grid=(rows // block,),
        in_specs=[
            pl.BlockSpec(memory_space=pltpu.SMEM),
            pl.BlockSpec((block, width), lambda i: (i, 0)),
            pl.BlockSpec((None, users, hist, width), lambda i: (layer, 0, 0, 0)),
            pl.BlockSpec((None, users, hist, width), lambda i: (layer, 0, 0, 0)),
        ],
        out_specs=pl.BlockSpec((block, width), lambda i: (i, 0)),
        scratch_shapes=[pltpu.VMEM((users, hist, width), BF)],
        compiler_params=pltpu.CompilerParams(vmem_limit_bytes=40 * 1024 * 1024),
        cost_estimate=pl.CostEstimate(
            flops=4 * rows * hist * width,
            bytes_accessed=4 * rows * width + 4 * users * hist * width,
            transcendentals=rows * hist * width // DH,
        ),
    )(lengths, x, keys, values)


def hop(x, k):
    return lax.ppermute(x, "tensor", [(i, i ^ k) for i in range(4)])


def absolute(rel, me):
    low = (me % 2) == 1
    high = (me // 2) == 1
    one = [jnp.where(low, rel[k ^ 1], rel[k]) for k in range(4)]
    return [jnp.where(high, one[k ^ 2], one[k]) for k in range(4)]


def gather_tensor(x):
    across = hop(x, 2)
    pair = jnp.stack([x, across])
    other = hop(pair, 1)
    return [x, other[0], across, other[1]]


def normalise(x):
    width = x.shape[1]
    total = jnp.sum(x, axis=1, keepdims=True)
    squares = jnp.sum(x * x, axis=1, keepdims=True)
    center = total / width
    spread = squares / width - center * center
    return (x - center) * lax.rsqrt(spread + EPS)


def dot(a, b):
    return jnp.dot(a, b, preferred_element_type=F32)


def per_device(candidates, candidate_user, history_lengths, w_in, w_out, hist_keys, hist_values):
    count, width = candidates.shape
    users = history_lengths.shape[0]
    owners = lax.axis_size("cache")
    me = lax.axis_index("tensor")
    heads = width // DH
    chunk = count // 4
    half_scale = DH ** (-0.5)

    user = candidate_user[:, 0]
    place = jnp.arange(count, dtype=jnp.int32)
    same = user[None, :] == user[:, None]
    less = user[None, :] < user[:, None]
    before = place[None, :] < place[:, None]
    rank = jnp.sum(same & before, axis=1, dtype=jnp.int32)
    position = jnp.sum(less, axis=1, dtype=jnp.int32) + rank
    part, index = position % 4, position // 4
    inner = (user % users) * 4 + rank // 4
    owner = user // users
    wide_slot = owner * 32 + part * 8 + inner
    slot = owner * 8 + inner
    slots_wide = owners * 32
    slots = owners * 8
    wide_table = (jnp.arange(slots_wide, dtype=jnp.int32)[:, None] == wide_slot[None, :]).astype(BF)
    slot_table = (jnp.arange(slots, dtype=jnp.int32)[:, None] == slot[None, :]).astype(BF)
    order = part * chunk + index
    order_table = (place[:, None] == order[None, :]).astype(BF)
    pick = (
        (jnp.arange(chunk, dtype=jnp.int32)[:, None] == index[None, :]) & (part == me)[None, :]
    ).astype(BF)
    table = lax.dot_general(
        slot_table, pick, (((1,), (1,)), ((), ())), preferred_element_type=F32
    ).astype(BF)

    def own_and_gate(normed, layer, q):
        rest = jnp.concatenate([w_in[layer, :, 0], w_in[layer, :, 1], w_in[layer, :, 3]], axis=1)
        pieces = silu(dot(normed, rest)).astype(BF)
        gate, value, key = pieces[:, :width], pieces[:, width : 2 * width], pieces[:, 2 * width :]
        qk = (q.astype(F32) * key.astype(F32)).reshape(count, heads, DH)
        weight = silu(jnp.sum(qk, axis=2) * half_scale)
        own = (weight[:, :, None] * value.astype(F32).reshape(count, heads, DH)).reshape(count, width)
        return gate, own.astype(BF)

    def rows_of(both):
        blocks = [both[k * chunk : (k + 1) * chunk] for k in range(4)]
        send = absolute(blocks, me)
        return absolute([send[0]] + [hop(send[k], k) for k in (1, 2, 3)], me)

    def finish(layer, state, history, gate, own, out_full):
        back = lax.all_to_all(history, ("cache", "tensor"), split_axis=0, concat_axis=0, tiled=True)
        back = back.reshape(owners, 4, 8, width).transpose(0, 2, 1, 3).reshape(slots, 4 * width)
        part_hist = lax.dot_general(
            table, back, (((0,), (0,)), ((), ())), preferred_element_type=F32
        )
        attention = (part_hist + own.astype(F32)).astype(BF).astype(F32)
        gated = (normalise(attention) * gate.astype(F32)).astype(BF)
        return (state.astype(F32) + dot(gated, out_full)).astype(BF)

    def split(both):
        gate = jnp.concatenate([b[:, :width] for b in both], axis=1)
        own = jnp.concatenate([b[:, width:] for b in both], axis=1)
        return gate, own

    full = jnp.concatenate(absolute(gather_tensor(candidates), me), axis=1)
    normed = normalise(full.astype(F32)).astype(BF)
    q = silu(dot(normed, w_in[0, :, 2])).astype(BF)
    placed = dot(wide_table, q).astype(BF)
    arrived = lax.all_to_all(
        placed.reshape(owners, 32, width), "cache", split_axis=0, concat_axis=0, tiled=True
    )
    gate, own = own_and_gate(normed, 0, q)
    both = dot(order_table, jnp.concatenate([gate, own], axis=1)).astype(BF)
    gate, own = split(rows_of(both))
    state = dot(pick, full).astype(BF)
    out_full = jnp.concatenate(absolute(gather_tensor(w_out[0]), me), axis=0)
    history = attend(0, history_lengths, arrived.reshape(-1, width), hist_keys, hist_values)
    history = history.reshape(owners * 4, 8, width)
    wq = jnp.concatenate(absolute(gather_tensor(w_in[1, :, 2]), me), axis=1)
    out_full_1 = jnp.concatenate(absolute(gather_tensor(w_out[1]), me), axis=0)
    state = finish(0, state, history, gate, own, out_full)

    normed = normalise(state.astype(F32)).astype(BF)
    q = silu(dot(normed, wq)).astype(BF)
    placed = dot(table, q).astype(BF)
    placed = placed.reshape(owners, 8, 4, width).transpose(0, 2, 1, 3).reshape(owners * 4, 8, width)
    arrived = lax.all_to_all(placed, ("cache", "tensor"), split_axis=0, concat_axis=0, tiled=True)
    normed_all = jnp.concatenate(absolute(gather_tensor(normed), me), axis=0)
    q_own = silu(dot(normed_all, w_in[1, :, 2])).astype(BF)
    gate, own = own_and_gate(normed_all, 1, q_own)
    gate, own = split(rows_of(jnp.concatenate([gate, own], axis=1)))
    history = attend(1, history_lengths, arrived.reshape(-1, width), hist_keys, hist_values)
    history = history.reshape(owners * 4, 8, width)
    state = finish(1, state, history, gate, own, out_full_1)

    cols = absolute([state[:, k * width : (k + 1) * width] for k in range(4)], me)
    result = absolute([cols[0]] + [hop(cols[k], k) for k in (1, 2, 3)], me)
    result = jnp.concatenate(result, axis=0)
    return lax.dot_general(
        order_table, result, (((0,), (0,)), ((), ())), preferred_element_type=F32
    ).astype(BF)


def solution(mesh):
    placed = (
        P("cache", "tensor"),
        P("cache", None),
        P("cache"),
        P(None, None, None, "tensor"),
        P(None, "tensor", None),
        P(None, "cache", None, "tensor"),
        P(None, "cache", None, "tensor"),
    )
    return jax.shard_map(
        per_device, mesh=mesh, in_specs=placed, out_specs=P("cache", "tensor"), check_vma=False
    )
```

```python
import jax
import jax.numpy as jnp
from jax import lax
from jax.experimental import pallas as pl
from jax.experimental.pallas import tpu as pltpu
from jax.sharding import PartitionSpec as P

DH = 128
EPS = 1e-05
BF = jnp.bfloat16
F32 = jnp.float32
I32 = jnp.int32
MIB = 1024 * 1024
SMEM = pl.BlockSpec(memory_space=pltpu.SMEM)
VMEM = pl.BlockSpec(memory_space=pltpu.VMEM)
TENSOR = 4
USERS = 2


def dot(a, b):
    return jnp.dot(a, b, preferred_element_type=F32)


def silu(x):
    half = 0.5 * x
    return half * jnp.tanh(half) + half


def iota(shape, axis):
    return lax.broadcasted_iota(I32, shape, axis)


def moments(parts, width):
    total = sum(jnp.sum(p, axis=1, keepdims=True) for p in parts)
    squares = sum(jnp.sum(p * p, axis=1, keepdims=True) for p in parts)
    center = total / width
    spread = squares / width - center * center
    return center, lax.rsqrt(spread + EPS)


def shaped(shape, dtype=BF):
    return jax.ShapeDtypeStruct(shape, dtype)


def call(kernel, name, outs, ins, *args, flops=1):
    return pl.pallas_call(
        kernel,
        out_shape=outs,
        in_specs=ins,
        out_specs=jax.tree.map(lambda _: VMEM, outs),
        compiler_params=pltpu.CompilerParams(vmem_limit_bytes=56 * MIB),
        cost_estimate=pl.CostEstimate(flops=flops, bytes_accessed=1, transcendentals=0),
        name=name,
    )(*args)


def slots(user, position, rank):
    return (user >> 1) * 32 + (position & 3) * 8 + (user & 1) * 4 + (rank >> 2)


def place_kernel(row_ref, col_ref, x_ref, out_ref, ids_ref):
    row, col = row_ref[...], col_ref[...]
    count = row.shape[1]
    step = 128
    zero = jnp.zeros((), F32)
    one = jnp.ones((), F32)

    def tally(mask, axis):
        return jnp.sum(jnp.where(mask, one, zero), axis=axis, keepdims=True)

    less = jnp.zeros((1, count), F32)
    ahead = jnp.zeros((1, count), F32)
    for r in range(0, count, step):
        mine = col[r : r + step]
        here = iota((step, count), 0) + r
        there = iota((step, count), 1)
        less = less + tally(mine < row, 0)
        ahead = ahead + tally((mine == row) & (here < there), 0)
        col_less = tally(row < mine, 1).astype(I32)
        col_rank = tally((mine == row) & (there < here), 1).astype(I32)
        ids_ref[r : r + step, :] = slots(mine, col_less + col_rank, col_rank)
    rank = ahead.astype(I32)
    slot = slots(row, less.astype(I32) + rank, rank)
    for s in range(0, out_ref.shape[0], 256):
        table = (iota((256, count), 0) + s == slot).astype(BF)
        out_ref[s : s + 256, :] = dot(table, x_ref[...]).astype(BF)


def place(user, x):
    count, width = x.shape
    outs = (shaped((2 * count, width)), shaped((count, 1), I32))
    return call(place_kernel, "place", outs, [VMEM] * 3, user.reshape(1, count), user, x)


def collect_kernel(ids, back, out_ref):
    count = out_ref.shape[0]
    for r in range(0, count, 256):
        table = (iota((256, back.shape[0]), 1) == ids[r : r + 256, :]).astype(BF)
        out_ref[r : r + 256, :] = dot(table, back[...]).astype(BF)


def collect(ids, back):
    outs = shaped((ids.shape[0], back.shape[1]))
    return call(collect_kernel, "collect", outs, [VMEM] * 2, ids, back)


def unpack(x_ref, state_ref):
    rows, model = state_ref.shape
    width = model // TENSOR
    a, b = iota((128, 512), 0), iota((128, 512), 1)
    for t in range(TENSOR):
        wanted = ((a >> 2) & 15) * 32 + t * 8 + (a >> 6) * 4 + (a & 3)
        table = (wanted == b).astype(BF)
        for n in range(rows // 128):
            got = dot(table, x_ref[n * 512 : (n + 1) * 512, :]).astype(BF)
            for u in range(USERS):
                here = u * (rows // USERS) + n * 64
                state_ref[here : here + 64, t * width : (t + 1) * width] = got[u * 64 : u * 64 + 64]


def pack(state_ref, out_ref):
    rows, model = state_ref.shape
    width = model // TENSOR
    a, b = iota((512, 512), 0), iota((512, 512), 1)
    wanted = ((a >> 3) & 3) * 128 + ((a >> 2) & 1) * 64 + (a >> 5) * 4 + (a & 3)
    table = (wanted == b).astype(BF)
    for n in range(rows // 128):
        parts = []
        for t in range(TENSOR):
            for u in range(USERS):
                here = u * (rows // USERS) + n * 64
                parts.append(state_ref[here : here + 64, t * width : (t + 1) * width])
        out_ref[n * 512 : (n + 1) * 512, :] = dot(table, jnp.concatenate(parts, axis=0)).astype(BF)


def wdot(x, pieces, cols):
    total, row = 0.0, 0
    for p in pieces:
        size = p.shape[0]
        total = total + dot(x[:, row : row + size], p[:, cols])
        row += size
    return total


def fetch(pairs, sems):
    copies = [
        pltpu.make_async_copy(src, dst, sems.at[i]) for i, (src, dst) in enumerate(pairs)
    ]
    for c in copies:
        c.start()
    return copies


def project(state, weights, normed_ref, outs):
    state = state.astype(F32)
    center, scale = moments([state], state.shape[1])
    normed = ((state - center) * scale).astype(BF)
    normed_ref[...] = normed
    half = normed.shape[0] // USERS
    for k in range(TENSOR):
        q = silu(wdot(normed, weights[k], slice(None))).astype(BF)
        for u in range(USERS):
            outs[u * TENSOR + k][...] = q[u * half : (u + 1) * half]


def query_specs(weights):
    return [
        pl.BlockSpec((p.shape[0], p.shape[1] // 4), lambda i: (0, 2)) for k in weights for p in k
    ]


def whole(x):
    return pl.BlockSpec(x.shape, lambda i: (0,) * len(x.shape))


def row_call(kernel, name, rows, width, args, weights):
    full = shaped((rows, TENSOR * width))
    outs = (full, full) + (shaped((rows // USERS, width)),) * (USERS * TENSOR)
    state, normed, *q = pl.pallas_call(
        kernel,
        out_shape=outs,
        grid=(1,),
        in_specs=[whole(a) for a in args] + query_specs(weights),
        out_specs=tuple(whole(o) for o in outs),
        compiler_params=pltpu.CompilerParams(vmem_limit_bytes=56 * MIB),
        cost_estimate=pl.CostEstimate(flops=1, bytes_accessed=1, transcendentals=0),
        name=name,
    )(*args, *[p for k in weights for p in k])
    return state, normed, (q[:TENSOR], q[TENSOR:])


def grouped(refs):
    size = len(refs) // TENSOR
    return [refs[k * size : (k + 1) * size] for k in range(TENSOR)]


def first(x, weights):
    count, width = x.shape
    pieces = sum(len(k) for k in weights)

    def kernel(x_ref, *refs):
        state_ref, normed_ref, *outs = refs[pieces:]
        unpack(x_ref, state_ref)
        project(state_ref[...], grouped(refs[:pieces]), normed_ref, outs)

    return row_call(kernel, "first", count // TENSOR, width, [x], weights)


def own(normed, q, weights):
    rows, model = normed.shape
    width = model // TENSOR
    flat = [p for k in weights for p in k]
    queries = [x for user in q for x in user]
    n = len(flat)

    def kernel(n_ref, *refs):
        q_refs, w_refs = refs[: USERS * TENSOR], refs[USERS * TENSOR : USERS * TENSOR + n]
        gate_ref, own_ref, *held, sems = refs[USERS * TENSOR + n :]
        copies = fetch(list(zip(w_refs, held)), sems)
        normed = n_ref[...]
        size = n // TENSOR
        for k in range(TENSOR):
            for c in copies[k * size : (k + 1) * size]:
                c.wait()
            pieces = held[k * size : (k + 1) * size]
            cols = slice(k * width, (k + 1) * width)
            gate, value, key = [
                silu(wdot(normed, pieces, slice(p * width, (p + 1) * width))).astype(BF)
                for p in (0, 1, 3)
            ]
            gate_ref[:, cols] = gate
            query = jnp.concatenate([q_refs[u * TENSOR + k][...] for u in range(USERS)], axis=0)
            for h in range(0, width, DH):
                part = query[:, h : h + DH].astype(F32) * key[:, h : h + DH].astype(F32)
                weight = silu(jnp.sum(part, axis=1, keepdims=True) * DH ** (-0.5))
                own_ref[:, k * width + h : k * width + h + DH] = weight * value[
                    :, h : h + DH
                ].astype(F32)

    return pl.pallas_call(
        kernel,
        out_shape=(shaped((rows, model)), shaped((rows, model), F32)),
        in_specs=[VMEM] * (1 + USERS * TENSOR) + [pl.BlockSpec(memory_space=pl.ANY)] * n,
        out_specs=(VMEM, VMEM),
        scratch_shapes=[pltpu.VMEM(p.shape, BF) for p in flat] + [pltpu.SemaphoreType.DMA((n,))],
        compiler_params=pltpu.CompilerParams(vmem_limit_bytes=56 * MIB),
        cost_estimate=pl.CostEstimate(flops=1, bytes_accessed=1, transcendentals=0),
        name="own",
    )(normed, *queries, *flat)


def attend_kernel(u, len_ref, q0, q1, q2, q3, k_ref, v_ref, *refs):
    *outs, vm_ref = refs
    hist, width = vm_ref.shape
    vm_ref[...] = jnp.where(
        iota((hist, width), 0) < len_ref[u], v_ref[...], jnp.zeros((), BF)
    )
    scale = 0.5 * DH ** (-0.5)
    for pair in ((0, 1), (2, 3)):
        q = jnp.concatenate([(q0, q1, q2, q3)[k][...] for k in pair], axis=0)
        half = q.shape[0] // 2
        for h in range(0, width, DH):
            cols = slice(h, h + DH)
            s = lax.dot_general(
                q[:, cols], k_ref[:, cols], (((1,), (1,)), ((), ())), preferred_element_type=F32
            )
            s = s * scale
            w = (s * jnp.tanh(s) + s).astype(BF)
            got = dot(w, vm_ref[:, cols]).astype(BF)
            outs[pair[0]][:, cols] = got[:half]
            outs[pair[1]][:, cols] = got[half:]


def attend(layer, u, lengths, q, keys, values):
    rows, width = q[0].shape
    hist = keys.shape[2]
    history = pl.BlockSpec((None, None, hist, width), lambda i: (layer, u, 0, 0))
    block = pl.BlockSpec((rows, width), lambda i: (0, 0))
    return pl.pallas_call(
        lambda *refs: attend_kernel(u, *refs),
        out_shape=(shaped((rows, width)),) * TENSOR,
        grid=(1,),
        in_specs=[SMEM] + [block] * TENSOR + [history, history],
        out_specs=(block,) * TENSOR,
        scratch_shapes=[pltpu.VMEM((hist, width), BF)],
        compiler_params=pltpu.CompilerParams(vmem_limit_bytes=56 * MIB),
        cost_estimate=pl.CostEstimate(
            flops=8 * rows * TENSOR * hist * width, bytes_accessed=4 * hist * width, transcendentals=0
        ),
        name="attend",
    )(lengths, *q, keys, values)


def update(refs):
    state_ref, gate_ref, own_ref = refs[:3]
    hist, outs = refs[3:11], refs[11:15]
    width = hist[0].shape[1]
    model = state_ref.shape[1]
    attention = []
    for k in range(TENSOR):
        got = jnp.concatenate([hist[u * TENSOR + k][...] for u in range(USERS)], axis=0)
        got = got.astype(F32) + own_ref[:, k * width : (k + 1) * width]
        attention.append(got.astype(BF).astype(F32))
    center, scale = moments(attention, model)
    total = state_ref[...].astype(F32)
    for k, a in enumerate(attention):
        gated = (a - center) * scale * gate_ref[:, k * width : (k + 1) * width].astype(F32)
        total = total + dot(gated.astype(BF), outs[k][...])
    return total.astype(BF)


def middle(state, gate, own_part, hist, outs, weights):
    rows, width = state.shape[0], hist[0][0].shape[1]
    pieces = sum(len(k) for k in weights)

    def kernel(*refs):
        new = update(refs[:15])
        state_ref, normed_ref, *q = refs[15 + pieces :]
        state_ref[...] = new
        project(new, grouped(refs[15 : 15 + pieces]), normed_ref, q)

    args = [state, gate, own_part, *hist[0], *hist[1], *outs]
    return row_call(kernel, "middle", rows, width, args, weights)


def end_kernel(*refs):
    out_ref, state_ref = refs[15:]
    state_ref[...] = update(refs[:15])
    pack(state_ref, out_ref)


def end(state, gate, own_part, hist, outs):
    rows, width = state.shape[0], hist[0][0].shape[1]
    args = [state, gate, own_part, *hist[0], *hist[1], *outs]
    return pl.pallas_call(
        end_kernel,
        out_shape=shaped((TENSOR * rows, width)),
        in_specs=[VMEM] * 15,
        out_specs=VMEM,
        scratch_shapes=[pltpu.VMEM(state.shape, BF)],
        compiler_params=pltpu.CompilerParams(vmem_limit_bytes=56 * MIB),
        cost_estimate=pl.CostEstimate(flops=1, bytes_accessed=1, transcendentals=0),
        name="end",
    )(*args)


def hop(x, k):
    return lax.ppermute(x, "tensor", [(i, i ^ k) for i in range(TENSOR)])


def wrap(x):
    total = TENSOR * lax.axis_size("cache")
    return lax.ppermute(x, ("cache", "tensor"), [(i, i ^ 6) for i in range(total)])


def gather(x, direct, *after):
    across = hop(x, 2) if direct else wrap(x)
    if after:
        across = tie(across, *after)
    return [x, hop(x, 1), across, hop(across, 1)]


def gather_pieces(a, b, *after):
    return list(zip(gather(a, True, *after), gather(b, False, *after)))


def swap(blocks):
    return [blocks[0], hop(blocks[1], 1), hop(blocks[2], 2), hop(blocks[3], 3)]


def tie(x, *others):
    return lax.optimization_barrier((x,) + others)[0]


def exchange(x):
    shape = x.shape
    x = x.reshape((shape[0] // 8, 8, shape[1]))
    everyone = ("cache", "tensor")
    return lax.all_to_all(x, everyone, split_axis=0, concat_axis=0, tiled=True).reshape(shape)


def per_device(candidates, candidate_user, history_lengths, w_in, w_out, hist_keys, hist_values):
    def halves(layer, cut, after):
        w = tie(w_in, after)[layer]
        model = w.shape[0]
        return w[:cut].reshape(cut, model), w[cut:].reshape(model - cut, model)

    def attention(layer, u, q):
        return swap(attend(layer, u, history_lengths, q, hist_keys, hist_values))

    placed, ids = place(candidate_user, candidates)
    rows = exchange(placed)
    w0 = gather_pieces(*halves(0, 512, placed))
    a1, b1 = halves(1, 384, placed)
    across_a = hop(tie(a1, w0[2][0]), 2)
    across_b = wrap(tie(b1, w0[2][1]))
    rows, w0, a1, b1 = lax.optimization_barrier((rows, w0, a1, b1))

    wo0 = gather(tie(w_out, across_b)[0], False)
    state, normed, q = first(rows, w0)
    gate, own_part = own(normed, q, w0)
    q0, q1 = swap(q[0]), swap(q[1])
    q0, gate, own_part = lax.optimization_barrier((q0, gate, own_part))
    hist0 = attention(0, 0, q0)
    hist1 = attention(0, 1, q1)
    across_a, across_b, _ = lax.optimization_barrier((across_a, across_b, hist1[0]))
    w1 = [(a1, b1), (hop(a1, 1), hop(b1, 1)), (across_a, across_b)]
    w1.append((hop(across_a, 1), hop(across_b, 1)))
    state, normed, q = middle(state, gate, own_part, (hist0, hist1), wo0, w1)

    gate, own_part = own(normed, q, w1)
    q0, q1 = swap(q[0]), swap(q[1])
    q0, gate, own_part = lax.optimization_barrier((q0, gate, own_part))
    hist0 = attention(1, 0, q0)
    wo1 = gather(tie(w_out, normed)[1], False, hist0[0])
    hist1 = attention(1, 1, q1)
    out = end(state, gate, own_part, (hist0, hist1), wo1)
    return collect(ids, exchange(out))


def solution(mesh):
    placed = (
        P("cache", "tensor"),
        P("cache", None),
        P("cache"),
        P(None, None, None, "tensor"),
        P(None, "tensor", None),
        P(None, "cache", None, "tensor"),
        P(None, "cache", None, "tensor"),
    )
    return jax.shard_map(
        per_device, mesh=mesh, in_specs=placed, out_specs=P("cache", "tensor"), check_vma=False
    )
```

```python
import jax
import jax.numpy as jnp
from jax import lax
from jax.experimental import pallas as pl
from jax.experimental.pallas import tpu as pltpu
from jax.sharding import PartitionSpec as P

DH = 128
EPS = 1e-05
BF = jnp.bfloat16
F32 = jnp.float32
I32 = jnp.int32
MIB = 1024 * 1024
SMEM = pl.BlockSpec(memory_space=pltpu.SMEM)
VMEM = pl.BlockSpec(memory_space=pltpu.VMEM)
FAR = pl.BlockSpec(memory_space=pltpu.HBM)
LIMIT = pltpu.CompilerParams(vmem_limit_bytes=20 * MIB)
TENSOR = 4
GATE, VALUE, QUERY, KEY = 0, 1, 0, 1
USERS = 2


def dot(a, b):
    return jnp.dot(a, b, preferred_element_type=F32)


def silu(x):
    half = 0.5 * x
    return half * jnp.tanh(half) + half


def iota(shape, axis):
    return lax.broadcasted_iota(I32, shape, axis)


def moments(parts, width):
    total = sum(jnp.sum(p, axis=1, keepdims=True) for p in parts)
    squares = sum(jnp.sum(p * p, axis=1, keepdims=True) for p in parts)
    center = total / width
    spread = squares / width - center * center
    return center, lax.rsqrt(spread + EPS)


def shaped(shape, dtype=BF):
    return jax.ShapeDtypeStruct(shape, dtype)


def call(kernel, name, outs, ins, *args, flops=1):
    return pl.pallas_call(
        kernel,
        out_shape=outs,
        in_specs=ins,
        out_specs=jax.tree.map(lambda _: VMEM, outs),
        compiler_params=LIMIT,
        cost_estimate=pl.CostEstimate(flops=flops, bytes_accessed=1, transcendentals=0),
        name=name,
    )(*args)


def slots(user, position, rank):
    return (user >> 1) * 32 + (position & 3) * 8 + (user & 1) * 4 + (rank >> 2)


def place_kernel(row_ref, col_ref, x_ref, out_ref, ids_ref):
    row, col = row_ref[...], col_ref[...]
    count = row.shape[1]
    step = 128
    zero = jnp.zeros((), F32)
    one = jnp.ones((), F32)

    def tally(mask, axis):
        return jnp.sum(jnp.where(mask, one, zero), axis=axis, keepdims=True)

    less = jnp.zeros((1, count), F32)
    ahead = jnp.zeros((1, count), F32)
    for r in range(0, count, step):
        mine = col[r : r + step]
        here = iota((step, count), 0) + r
        there = iota((step, count), 1)
        less = less + tally(mine < row, 0)
        ahead = ahead + tally((mine == row) & (here < there), 0)
        col_less = tally(row < mine, 1).astype(I32)
        col_rank = tally((mine == row) & (there < here), 1).astype(I32)
        ids_ref[r : r + step, :] = slots(mine, col_less + col_rank, col_rank)
    rank = ahead.astype(I32)
    slot = slots(row, less.astype(I32) + rank, rank)
    for s in range(0, out_ref.shape[0], 256):
        table = (iota((256, count), 0) + s == slot).astype(BF)
        out_ref[s : s + 256, :] = dot(table, x_ref[...]).astype(BF)


def place(user, x):
    count, width = x.shape
    outs = (shaped((2 * count, width)), shaped((count, 1), I32))
    return call(place_kernel, "place", outs, [VMEM] * 3, user.reshape(1, count), user, x)


def collect_kernel(ids, back, out_ref):
    count = out_ref.shape[0]
    for r in range(0, count, 256):
        table = (iota((256, back.shape[0]), 1) == ids[r : r + 256, :]).astype(BF)
        out_ref[r : r + 256, :] = dot(table, back[...]).astype(BF)


def collect(ids, back):
    outs = shaped((ids.shape[0], back.shape[1]))
    return call(collect_kernel, "collect", outs, [VMEM] * 2, ids, back)


def unpack(x_ref, state_ref):
    rows, model = state_ref.shape
    width = model // TENSOR
    a, b = iota((128, 512), 0), iota((128, 512), 1)
    for t in range(TENSOR):
        wanted = ((a >> 2) & 15) * 32 + t * 8 + (a >> 6) * 4 + (a & 3)
        table = (wanted == b).astype(BF)
        for n in range(rows // 128):
            got = dot(table, x_ref[n * 512 : (n + 1) * 512, :]).astype(BF)
            for u in range(USERS):
                here = u * (rows // USERS) + n * 64
                state_ref[here : here + 64, t * width : (t + 1) * width] = got[u * 64 : u * 64 + 64]


def pack(state_ref, out_ref):
    rows, model = state_ref.shape
    width = model // TENSOR
    a, b = iota((512, 512), 0), iota((512, 512), 1)
    wanted = ((a >> 3) & 3) * 128 + ((a >> 2) & 1) * 64 + (a >> 5) * 4 + (a & 3)
    table = (wanted == b).astype(BF)
    for n in range(rows // 128):
        parts = []
        for t in range(TENSOR):
            for u in range(USERS):
                here = u * (rows // USERS) + n * 64
                parts.append(state_ref[here : here + 64, t * width : (t + 1) * width])
        out_ref[n * 512 : (n + 1) * 512, :] = dot(table, jnp.concatenate(parts, axis=0)).astype(BF)


def fetch(pairs, sems):
    copies = [
        pltpu.make_async_copy(src, dst, sems.at[i]) for i, (src, dst) in enumerate(pairs)
    ]
    for c in copies:
        c.start()
    return copies


def wait(copies):
    for c in copies:
        c.wait()


def project(state, copies, held, normed_ref, outs):
    state = state.astype(F32)
    center, scale = moments([state], state.shape[1])
    normed = ((state - center) * scale).astype(BF)
    normed_ref[...] = normed
    for k, out in enumerate(outs):
        copies[k].wait()
        out[...] = silu(dot(normed, held[k])).astype(BF)


def row_call(kernel, name, outs, args, far, held):
    return pl.pallas_call(
        kernel,
        out_shape=outs,
        in_specs=[VMEM] * len(args) + [FAR] * len(far),
        out_specs=jax.tree.map(lambda _: VMEM, outs),
        scratch_shapes=[pltpu.VMEM(h, BF) for h in held] + [pltpu.SemaphoreType.DMA((32,))],
        compiler_params=LIMIT,
        cost_estimate=pl.CostEstimate(flops=1, bytes_accessed=1, transcendentals=0),
        name=name,
    )(*args, *far)


def row_outs(rows, width):
    full = shaped((rows, TENSOR * width))
    return (full, full) + (shaped((rows, width)),) * TENSOR


def blocks(refs, part, held):
    return [(ref.at[part], held.at[k]) for k, ref in enumerate(refs)]


def first(x, queries):
    count, width = x.shape
    model = TENSOR * width

    def kernel(x_ref, *refs):
        state_ref, normed_ref, *outs, held, sems = refs[TENSOR:]
        copies = fetch(blocks(refs[:TENSOR], QUERY, held), sems)
        unpack(x_ref, state_ref)
        project(state_ref[...], copies, held, normed_ref, outs)

    outs = row_outs(count // TENSOR, width)
    held = [(TENSOR, model, width)]
    state, normed, *q = row_call(kernel, "first", outs, [x], queries, held)
    return state, normed, q


def own(normed, q, keys, values):
    rows, model = normed.shape
    width = model // TENSOR

    def kernel(n_ref, *refs):
        q_refs, key_refs, value_refs = refs[:4], refs[4:8], refs[8:12]
        own_ref, key_held, value_held, sems = refs[12:]
        copies = fetch(blocks(key_refs, KEY, key_held) + blocks(value_refs, VALUE, value_held), sems)
        normed = n_ref[...]
        for k in range(TENSOR):
            copies[k].wait()
            key = silu(dot(normed, key_held[k])).astype(BF).astype(F32)
            copies[TENSOR + k].wait()
            value = silu(dot(normed, value_held[k])).astype(BF).astype(F32)
            product = q_refs[k][...].astype(F32) * key
            for h in range(0, width, DH):
                score = jnp.sum(product[:, h : h + DH], axis=1, keepdims=True)
                weight = silu(score * DH ** (-0.5))
                own_ref[:, k * width + h : k * width + h + DH] = (
                    weight * value[:, h : h + DH]
                ).astype(BF)

    held = [(TENSOR, model, width)] * 2
    return row_call(kernel, "own", shaped((rows, model)), [normed, *q], [*keys, *values], held)


def gates(normed, weights):
    rows, model = normed.shape
    width = model // TENSOR

    def kernel(n_ref, *refs):
        gate_ref, held, sems = refs[TENSOR:]
        copies = fetch(blocks(refs[:TENSOR], GATE, held), sems)
        normed = n_ref[...]
        for k in range(TENSOR):
            copies[k].wait()
            gate_ref[:, k * width : (k + 1) * width] = silu(dot(normed, held[k])).astype(BF)

    held = [(TENSOR, model, width)]
    return row_call(kernel, "gates", shaped((rows, model)), [normed], weights, held)


def attend(layer, u, lengths, q, keys, values):
    rows, width = q[0].shape[0] // USERS, q[0].shape[1]
    hist = keys.shape[2]
    scale = 0.5 * DH ** (-0.5)

    def kernel(len_ref, q0, q1, q2, q3, k_ref, v_ref, *refs):
        *outs, keys_ref, values_ref, sems = refs
        first, second = fetch(
            [(k_ref.at[layer, u], keys_ref), (v_ref.at[layer, u], values_ref)], sems
        )
        mine = slice(u * rows, (u + 1) * rows)
        first.wait()
        masked = None
        for pair in ((0, 1), (2, 3)):
            q = jnp.concatenate([(q0, q1, q2, q3)[k][mine, :] for k in pair], axis=0)
            for h in range(0, width, DH):
                cols = slice(h, h + DH)
                s = lax.dot_general(
                    q[:, cols],
                    keys_ref[:, cols],
                    (((1,), (1,)), ((), ())),
                    preferred_element_type=F32,
                )
                s = s * scale
                w = (s * jnp.tanh(s) + s).astype(BF)
                if masked is None:
                    second.wait()
                    live = iota((hist, width), 0) < len_ref[u]
                    masked = jnp.where(live, values_ref[...], jnp.zeros((), BF))
                    values_ref[...] = masked
                got = dot(w, values_ref[:, cols]).astype(BF)
                outs[pair[0]][:, cols] = got[:rows]
                outs[pair[1]][:, cols] = got[rows:]

    return pl.pallas_call(
        kernel,
        out_shape=(shaped((rows, width)),) * TENSOR,
        in_specs=[SMEM] + [VMEM] * TENSOR + [FAR, FAR],
        out_specs=(VMEM,) * TENSOR,
        scratch_shapes=[pltpu.VMEM((hist, width), BF)] * 2 + [pltpu.SemaphoreType.DMA((2,))],
        compiler_params=LIMIT,
        cost_estimate=pl.CostEstimate(flops=1, bytes_accessed=1, transcendentals=0),
        name="attend",
    )(lengths, *q, keys, values)


def update(refs, copies, held):
    state_ref, gate_ref, own_ref = refs[:3]
    hist = refs[3:11]
    width = hist[0].shape[1]
    model = state_ref.shape[1]
    attention = []
    for k in range(TENSOR):
        got = jnp.concatenate([hist[u * TENSOR + k][...] for u in range(USERS)], axis=0)
        got = got.astype(F32) + own_ref[:, k * width : (k + 1) * width].astype(F32)
        attention.append(got.astype(BF).astype(F32))
    center, scale = moments(attention, model)
    gated = [
        ((a - center) * scale * gate_ref[:, k * width : (k + 1) * width].astype(F32)).astype(BF)
        for k, a in enumerate(attention)
    ]
    wait(copies)
    total = state_ref[...].astype(F32) + dot(jnp.concatenate(gated, axis=1), held[...])
    return total.astype(BF)


def out_rows(outs, held):
    width = outs[0].shape[0]
    return [(o, held.at[pl.ds(k * width, width)]) for k, o in enumerate(outs)]


def middle(state, gate, own_part, hist, outs, queries):
    rows, model = state.shape
    width = model // TENSOR

    def kernel(*refs):
        out_refs, query_refs = refs[11:15], refs[15:19]
        state_ref, normed_ref, *q, held_out, held, sems = refs[19:]
        copies = fetch(out_rows(out_refs, held_out) + blocks(query_refs, QUERY, held), sems)
        new = update(refs[:11], copies[:TENSOR], held_out)
        state_ref[...] = new
        project(new, copies[TENSOR:], held, normed_ref, q)

    args = [state, gate, own_part, *hist[0], *hist[1]]
    held = [(model, model), (TENSOR, model, width)]
    far = [*outs, *queries]
    state, normed, *q = row_call(kernel, "middle", row_outs(rows, width), args, far, held)
    return state, normed, q


def end(state, gate, own_part, hist, outs):
    rows, model = state.shape

    def kernel(*refs):
        out_ref, held, state_ref, sems = refs[15:]
        copies = fetch(out_rows(refs[11:15], held), sems)
        state_ref[...] = update(refs[:11], copies, held)
        pack(state_ref, out_ref)

    args = [state, gate, own_part, *hist[0], *hist[1]]
    out = shaped((TENSOR * rows, model // TENSOR))
    return row_call(kernel, "end", out, args, list(outs), [(model, model), state.shape])


def hop(x, k):
    return lax.ppermute(x, "tensor", [(i, i ^ k) for i in range(TENSOR)])


def wrap(x):
    total = TENSOR * lax.axis_size("cache")
    return lax.ppermute(x, ("cache", "tensor"), [(i, i ^ 6) for i in range(total)])


def spread(x, across, after):
    across = tie(across, after)
    return [x, hop(x, 1), across, hop(across, 1)]


def swap(blocks):
    return [blocks[0], hop(blocks[1], 1), hop(blocks[2], 2), hop(blocks[3], 3)]


def tie(x, *others):
    return lax.optimization_barrier((x,) + others)[0]


def exchange(x):
    shape = x.shape
    x = x.reshape((shape[0] // 8, 8, shape[1]))
    everyone = ("cache", "tensor")
    return lax.all_to_all(x, everyone, split_axis=0, concat_axis=0, tiled=True).reshape(shape)


def per_device(candidates, candidate_user, history_lengths, w_in, w_out, hist_keys, hist_values):
    def attention(number, u, q):
        return attend(number, u, history_lengths, q, hist_keys, hist_values)

    parts = w_in.transpose(0, 2, 1, 3)
    (gv0, qk0), (gv1, qk1) = [(parts[l, :2], parts[l, 2:]) for l in range(2)]
    far_qk0, far_gv0 = hop(qk0, 2), wrap(gv0)
    placed, ids = place(candidate_user, tie(candidates, qk0, gv0))
    rows = exchange(placed)
    qk0, gv0 = spread(qk0, far_qk0, placed), spread(gv0, far_gv0, placed)
    far_out0 = hop(tie(w_out, qk0[2])[0], 2)
    far_qk1 = wrap(tie(qk1, gv0[2]))
    rows, qk0, gv0 = lax.optimization_barrier((rows, qk0, gv0))

    state, normed, q = first(rows, qk0)
    part = own(normed, q, qk0, gv0)
    q, part = lax.optimization_barrier((swap(q), part))
    out0 = spread(w_out[0], far_out0, q[2])
    far_gv1 = wrap(tie(gv1, q[2]))
    a0 = attention(0, 0, q)
    qk1 = spread(qk1, far_qk1, a0[0])
    a1 = attention(0, 1, q)
    gate = gates(tie(normed, a1[0]), gv0)
    hist = swap(a0), swap(a1)
    state, normed, q = middle(state, gate, part, hist, out0, qk1)

    far_out1 = wrap(tie(w_out, normed)[1])
    gv1 = spread(gv1, far_gv1, normed)
    part = own(normed, q, qk1, gv1)
    q, part = lax.optimization_barrier((swap(q), part))
    a0 = attention(1, 0, q)
    out1 = spread(w_out[1], far_out1, a0[0])
    a1 = attention(1, 1, q)
    gate = gates(tie(normed, a1[0]), gv1)
    hist = swap(a0), swap(a1)
    out = end(state, gate, part, hist, out1)
    return collect(ids, exchange(out))


def solution(mesh):
    placed = (
        P("cache", "tensor"),
        P("cache", None),
        P("cache"),
        P(None, None, None, "tensor"),
        P(None, "tensor", None),
        P(None, "cache", None, "tensor"),
        P(None, "cache", None, "tensor"),
    )
    return jax.shard_map(
        per_device, mesh=mesh, in_specs=placed, out_specs=P("cache", "tensor"), check_vma=False
    )
```

```python
import jax
import jax.numpy as jnp
from jax import lax
from jax.experimental import pallas as pl
from jax.experimental.pallas import tpu as pltpu
from jax.sharding import PartitionSpec as P

DH = 128
EPS = 1e-05
BF = jnp.bfloat16
F32 = jnp.float32
I32 = jnp.int32
MIB = 1024 * 1024
SMEM = pl.BlockSpec(memory_space=pltpu.SMEM)
VMEM = pl.BlockSpec(memory_space=pltpu.VMEM)
FAR = pl.BlockSpec(memory_space=pltpu.HBM)
LIMIT = pltpu.CompilerParams(vmem_limit_bytes=20 * MIB)
TENSOR = 4
GATE, VALUE, QUERY, KEY = 0, 1, 0, 1
USERS = 2


def dot(a, b):
    return jnp.dot(a, b, preferred_element_type=F32)


def silu(x):
    half = 0.5 * x
    return half * jnp.tanh(half) + half


def iota(shape, axis):
    return lax.broadcasted_iota(I32, shape, axis)


def moments(parts, width):
    total = sum(jnp.sum(p, axis=1, keepdims=True) for p in parts)
    squares = sum(jnp.sum(p * p, axis=1, keepdims=True) for p in parts)
    center = total / width
    spread = squares / width - center * center
    return center, lax.rsqrt(spread + EPS)


def shaped(shape, dtype=BF):
    return jax.ShapeDtypeStruct(shape, dtype)


def call(kernel, name, outs, ins, *args, flops=1):
    return pl.pallas_call(
        kernel,
        out_shape=outs,
        in_specs=ins,
        out_specs=jax.tree.map(lambda _: VMEM, outs),
        compiler_params=LIMIT,
        cost_estimate=pl.CostEstimate(flops=flops, bytes_accessed=1, transcendentals=0),
        name=name,
    )(*args)


def slots(user, position, rank):
    return (user >> 1) * 32 + (position & 3) * 8 + (user & 1) * 4 + (rank >> 2)


def column(row, start):
    piece = row[:, start : start + 128].astype(F32)
    diagonal = iota((128, 128), 0) == iota((128, 128), 1)
    return jnp.sum(jnp.where(diagonal, piece, jnp.zeros((), F32)), axis=1, keepdims=True).astype(I32)


def place_kernel(row_ref, x_ref, out_ref, ids_ref):
    row = row_ref[...]
    count = row.shape[1]
    step = 128
    zero = jnp.zeros((), F32)
    one = jnp.ones((), F32)

    def tally(mask):
        return jnp.sum(jnp.where(mask, one, zero), axis=0, keepdims=True)

    less = jnp.zeros((1, count), F32)
    ahead = jnp.zeros((1, count), F32)
    for r in range(0, count, step):
        mine = column(row, r)
        here = iota((step, count), 0) + r
        there = iota((step, count), 1)
        less = less + tally(mine < row)
        ahead = ahead + tally((mine == row) & (here < there))
    rank = ahead.astype(I32)
    slot = slots(row, less.astype(I32) + rank, rank)
    ids_ref[...] = slot
    for s in range(0, out_ref.shape[0], 256):
        table = (iota((256, count), 0) + s == slot).astype(BF)
        out_ref[s : s + 256, :] = dot(table, x_ref[...]).astype(BF)


def place(user, x):
    count, width = x.shape
    outs = (shaped((2 * count, width)), shaped((1, count), I32))
    return call(place_kernel, "place", outs, [VMEM] * 2, user.reshape(1, count), x)


def collect_kernel(ids_ref, back, out_ref):
    count = out_ref.shape[0]
    ids = ids_ref[...]
    for r in range(0, count, 256):
        mine = jnp.concatenate([column(ids, r), column(ids, r + 128)], axis=0)
        table = (iota((256, back.shape[0]), 1) == mine).astype(BF)
        out_ref[r : r + 256, :] = dot(table, back[...]).astype(BF)


def collect(ids, back):
    outs = shaped((ids.shape[1], back.shape[1]))
    return call(collect_kernel, "collect", outs, [VMEM] * 2, ids, back)


def unpack(x_ref, state_ref):
    rows, model = state_ref.shape
    width = model // TENSOR
    a, b = iota((512, 512), 0), iota((512, 512), 1)
    wanted = ((a >> 2) & 15) * 32 + (a >> 7) * 8 + ((a >> 6) & 1) * 4 + (a & 3)
    table = (wanted == b).astype(BF)
    for n in range(rows // 128):
        got = dot(table, x_ref[n * 512 : (n + 1) * 512, :]).astype(BF)
        for t in range(TENSOR):
            for u in range(USERS):
                here, there = u * (rows // USERS) + n * 64, t * 128 + u * 64
                state_ref[here : here + 64, t * width : (t + 1) * width] = got[there : there + 64]


def pack(state_ref, out_ref):
    rows, model = state_ref.shape
    width = model // TENSOR
    a, b = iota((512, 512), 0), iota((512, 512), 1)
    wanted = ((a >> 3) & 3) * 128 + ((a >> 2) & 1) * 64 + (a >> 5) * 4 + (a & 3)
    table = (wanted == b).astype(BF)
    for n in range(rows // 128):
        parts = []
        for t in range(TENSOR):
            for u in range(USERS):
                here = u * (rows // USERS) + n * 64
                parts.append(state_ref[here : here + 64, t * width : (t + 1) * width])
        out_ref[n * 512 : (n + 1) * 512, :] = dot(table, jnp.concatenate(parts, axis=0)).astype(BF)


def fetch(pairs, sems):
    copies = [
        pltpu.make_async_copy(src, dst, sems.at[i]) for i, (src, dst) in enumerate(pairs)
    ]
    for c in copies:
        c.start()
    return copies


def wait(copies):
    for c in copies:
        c.wait()


def project(state, copies, held, normed_ref, outs):
    state = state.astype(F32)
    center, scale = moments([state], state.shape[1])
    normed = ((state - center) * scale).astype(BF)
    normed_ref[...] = normed
    half = normed.shape[0] // USERS
    for k in range(TENSOR):
        copies[k].wait()
        q = silu(dot(normed, held[k])).astype(BF)
        for u in range(USERS):
            outs[u * TENSOR + k][...] = q[u * half : (u + 1) * half]


def row_call(kernel, name, outs, args, far, held, flops=1):
    return pl.pallas_call(
        kernel,
        out_shape=outs,
        in_specs=[VMEM] * len(args) + [FAR] * len(far),
        out_specs=jax.tree.map(lambda _: VMEM, outs),
        scratch_shapes=[pltpu.VMEM(h, BF) for h in held] + [pltpu.SemaphoreType.DMA((32,))],
        compiler_params=LIMIT,
        cost_estimate=pl.CostEstimate(flops=flops, bytes_accessed=1, transcendentals=0),
        name=name,
    )(*args, *far)


def row_outs(rows, width):
    full = shaped((rows, TENSOR * width))
    return (full, full) + (shaped((rows // USERS, width)),) * (USERS * TENSOR)


def blocks(refs, part, held):
    return [(ref.at[part], held.at[k]) for k, ref in enumerate(refs)]


def first(x, queries):
    count, width = x.shape
    model = TENSOR * width

    def kernel(x_ref, *refs):
        state_ref, normed_ref, *outs, held, sems = refs[TENSOR:]
        copies = fetch(blocks(refs[:TENSOR], QUERY, held), sems)
        unpack(x_ref, state_ref)
        project(state_ref[...], copies, held, normed_ref, outs)

    outs = row_outs(count // TENSOR, width)
    held = [(TENSOR, model, width)]
    state, normed, *q = row_call(kernel, "first", outs, [x], queries, held)
    return state, normed, (q[:TENSOR], q[TENSOR:])


def own(normed, q, keys, values):
    rows, model = normed.shape
    width = model // TENSOR

    def kernel(n_ref, *refs):
        q_refs, key_refs, value_refs = refs[:8], refs[8:12], refs[12:16]
        own_ref, key_held, value_held, sems = refs[16:]
        copies = fetch(blocks(key_refs, KEY, key_held) + blocks(value_refs, VALUE, value_held), sems)
        normed = n_ref[...]
        for k in range(TENSOR):
            copies[k].wait()
            key = silu(dot(normed, key_held[k])).astype(BF).astype(F32)
            copies[TENSOR + k].wait()
            value = silu(dot(normed, value_held[k])).astype(BF).astype(F32)
            query = jnp.concatenate([q_refs[u * TENSOR + k][...] for u in range(USERS)], axis=0)
            product = query.astype(F32) * key
            for h in range(0, width, DH):
                score = jnp.sum(product[:, h : h + DH], axis=1, keepdims=True)
                weight = silu(score * DH ** (-0.5))
                own_ref[:, k * width + h : k * width + h + DH] = (
                    weight * value[:, h : h + DH]
                ).astype(BF)

    held = [(TENSOR, model, width)] * 2
    return row_call(kernel, "own", shaped((rows, model)), [normed, *q[0], *q[1]], [*keys, *values], held)


def gates(normed, weights):
    rows, model = normed.shape
    width = model // TENSOR

    def kernel(n_ref, *refs):
        gate_ref, held, sems = refs[TENSOR:]
        copies = fetch(blocks(refs[:TENSOR], GATE, held), sems)
        normed = n_ref[...]
        for k in range(TENSOR):
            copies[k].wait()
            gate_ref[:, k * width : (k + 1) * width] = silu(dot(normed, held[k])).astype(BF)

    held = [(TENSOR, model, width)]
    outs = shaped((rows, model))
    return row_call(kernel, "gates", outs, [normed], weights, held, flops=8 * rows * model * model)


def attend(layer, u, lengths, q, keys, values):
    rows, width = q[0].shape
    hist = keys.shape[2]
    scale = 0.5 * DH ** (-0.5)

    def kernel(len_ref, q0, q1, q2, q3, k_ref, v_ref, *refs):
        *outs, keys_ref, values_ref, sems = refs
        first, second = fetch(
            [(k_ref.at[layer, u], keys_ref), (v_ref.at[layer, u], values_ref)], sems
        )
        first.wait()
        masked = None
        for pair in ((0, 1), (2, 3)):
            q = jnp.concatenate([(q0, q1, q2, q3)[k][...] for k in pair], axis=0)
            for h in range(0, width, DH):
                cols = slice(h, h + DH)
                s = lax.dot_general(
                    q[:, cols],
                    keys_ref[:, cols],
                    (((1,), (1,)), ((), ())),
                    preferred_element_type=F32,
                )
                s = s * scale
                w = (s * jnp.tanh(s) + s).astype(BF)
                if masked is None:
                    second.wait()
                    live = iota((hist, width), 0) < len_ref[u]
                    masked = jnp.where(live, values_ref[...], jnp.zeros((), BF))
                    values_ref[...] = masked
                got = dot(w, values_ref[:, cols]).astype(BF)
                outs[pair[0]][:, cols] = got[:rows]
                outs[pair[1]][:, cols] = got[rows:]

    return pl.pallas_call(
        kernel,
        out_shape=(shaped((rows, width)),) * TENSOR,
        in_specs=[SMEM] + [VMEM] * TENSOR + [FAR, FAR],
        out_specs=(VMEM,) * TENSOR,
        scratch_shapes=[pltpu.VMEM((hist, width), BF)] * 2 + [pltpu.SemaphoreType.DMA((2,))],
        compiler_params=LIMIT,
        cost_estimate=pl.CostEstimate(flops=1, bytes_accessed=1, transcendentals=0),
        name="attend",
    )(lengths, *q, keys, values)


def update(refs, copies, held):
    state_ref, gate_ref, own_ref = refs[:3]
    hist = refs[3:11]
    width = hist[0].shape[1]
    model = state_ref.shape[1]
    attention = []
    for k in range(TENSOR):
        got = jnp.concatenate([hist[u * TENSOR + k][...] for u in range(USERS)], axis=0)
        got = got.astype(F32) + own_ref[:, k * width : (k + 1) * width].astype(F32)
        attention.append(got.astype(BF).astype(F32))
    center, scale = moments(attention, model)
    gated = [
        ((a - center) * scale * gate_ref[:, k * width : (k + 1) * width].astype(F32)).astype(BF)
        for k, a in enumerate(attention)
    ]
    wait(copies)
    total = state_ref[...].astype(F32) + dot(jnp.concatenate(gated, axis=1), held[...])
    return total.astype(BF)


def out_rows(outs, held):
    width = outs[0].shape[0]
    return [(o, held.at[pl.ds(k * width, width)]) for k, o in enumerate(outs)]


def middle(state, gate, own_part, hist, outs, queries):
    rows, model = state.shape
    width = model // TENSOR

    def kernel(*refs):
        out_refs, query_refs = refs[11:15], refs[15:19]
        state_ref, normed_ref, *q, held_out, held, sems = refs[19:]
        copies = fetch(out_rows(out_refs, held_out) + blocks(query_refs, QUERY, held), sems)
        new = update(refs[:11], copies[:TENSOR], held_out)
        state_ref[...] = new
        project(new, copies[TENSOR:], held, normed_ref, q)

    args = [state, gate, own_part, *hist[0], *hist[1]]
    held = [(model, model), (TENSOR, model, width)]
    far = [*outs, *queries]
    state, normed, *q = row_call(kernel, "middle", row_outs(rows, width), args, far, held)
    return state, normed, (q[:TENSOR], q[TENSOR:])


def end(state, gate, own_part, hist, outs):
    rows, model = state.shape

    def kernel(*refs):
        out_ref, held, state_ref, sems = refs[15:]
        copies = fetch(out_rows(refs[11:15], held), sems)
        state_ref[...] = update(refs[:11], copies, held)
        pack(state_ref, out_ref)

    args = [state, gate, own_part, *hist[0], *hist[1]]
    out = shaped((TENSOR * rows, model // TENSOR))
    return row_call(kernel, "end", out, args, list(outs), [(model, model), state.shape])


def hop(x, k):
    return lax.ppermute(x, "tensor", [(i, i ^ k) for i in range(TENSOR)])


def wrap(x):
    total = TENSOR * lax.axis_size("cache")
    return lax.ppermute(x, ("cache", "tensor"), [(i, i ^ 6) for i in range(total)])


def spread(x, beside, across, after):
    across = tie(across, after)
    return [x, beside, across, hop(across, 1)]


def swap(blocks):
    return [blocks[0], hop(blocks[1], 1), hop(blocks[2], 2), hop(blocks[3], 3)]


def tie(x, *others):
    return lax.optimization_barrier((x,) + others)[0]


def exchange(x):
    shape = x.shape
    x = x.reshape((shape[0] // 8, 8, shape[1]))
    everyone = ("cache", "tensor")
    return lax.all_to_all(x, everyone, split_axis=0, concat_axis=0, tiled=True).reshape(shape)


def per_device(candidates, candidate_user, history_lengths, w_in, w_out, hist_keys, hist_values):
    def attention(number, u, q):
        return attend(number, u, history_lengths, q, hist_keys, hist_values)

    parts = w_in.transpose(0, 2, 1, 3)
    (gv0, qk0), (gv1, qk1) = [(parts[l, :2], parts[l, 2:]) for l in range(2)]
    far_qk0, far_gv0 = hop(qk0, 2), wrap(gv0)
    placed, ids = place(candidate_user, tie(candidates, qk0, gv0))
    rows = exchange(placed)
    beside = [hop(tie(x, placed), 1) for x in (qk0, gv0, qk1, gv1, w_out)]
    qk0 = spread(qk0, beside[0], far_qk0, placed)
    gv0 = spread(gv0, beside[1], far_gv0, placed)
    far_qk1 = wrap(tie(qk1, gv0[2]))
    rows, qk0, gv0, beside = lax.optimization_barrier((rows, qk0, gv0, beside))

    state, normed, q = first(rows, qk0)
    part = own(normed, q, qk0, gv0)
    q0, q1 = swap(q[0]), swap(q[1])
    q0, part = lax.optimization_barrier((q0, part))
    far_out0 = wrap(tie(w_out, q0[2])[0])
    far_gv1 = wrap(tie(gv1, q0[2]))
    a0 = attention(0, 0, q0)
    qk1 = spread(qk1, beside[2], far_qk1, a0[0])
    q1, _ = lax.optimization_barrier((q1, a0[0]))
    a1 = attention(0, 1, q1)
    out0 = spread(w_out[0], beside[4][0], far_out0, a1[0])
    gate = gates(tie(normed, a1[0]), gv0)
    hist = swap(a0), swap(a1)
    state, normed, q = middle(state, gate, part, hist, out0, qk1)

    gv1 = spread(gv1, beside[3], far_gv1, normed)
    part = own(normed, q, qk1, gv1)
    q0, q1 = swap(q[0]), swap(q[1])
    q0, part = lax.optimization_barrier((q0, part))
    far_out1 = wrap(tie(w_out, q0[2])[1])
    a0 = attention(1, 0, q0)
    q1, _ = lax.optimization_barrier((q1, a0[0]))
    a1 = attention(1, 1, q1)
    out1 = spread(w_out[1], beside[4][1], far_out1, a1[0])
    gate = gates(tie(normed, a1[0]), gv1)
    hist = swap(a0), swap(a1)
    out = end(state, gate, part, hist, out1)
    return collect(ids, exchange(out))


def solution(mesh):
    placed = (
        P("cache", "tensor"),
        P("cache", None),
        P("cache"),
        P(None, None, None, "tensor"),
        P(None, "tensor", None),
        P(None, "cache", None, "tensor"),
        P(None, "cache", None, "tensor"),
    )
    return jax.shard_map(
        per_device, mesh=mesh, in_specs=placed, out_specs=P("cache", "tensor"), check_vma=False
    )
```

```python
import jax
import jax.numpy as jnp
from jax import lax
from jax.experimental import pallas as pl
from jax.experimental.pallas import tpu as pltpu
from jax.sharding import PartitionSpec as P

DH = 128
EPS = 1e-05
BF = jnp.bfloat16
F32 = jnp.float32
I32 = jnp.int32
MIB = 1024 * 1024
SMEM = pl.BlockSpec(memory_space=pltpu.SMEM)
VMEM = pl.BlockSpec(memory_space=pltpu.VMEM)
FAR = pl.BlockSpec(memory_space=pltpu.HBM)
LIMIT = pltpu.CompilerParams(vmem_limit_bytes=20 * MIB)
TENSOR = 4
GATE, VALUE, QUERY, KEY = 0, 1, 0, 1
USERS = 2


def dot(a, b):
    return jnp.dot(a, b, preferred_element_type=F32)


def silu(x):
    half = 0.5 * x
    return half * jnp.tanh(half) + half


def iota(shape, axis):
    return lax.broadcasted_iota(I32, shape, axis)


def moments(parts, width):
    total = sum(jnp.sum(p, axis=1, keepdims=True) for p in parts)
    squares = sum(jnp.sum(p * p, axis=1, keepdims=True) for p in parts)
    center = total / width
    spread = squares / width - center * center
    return center, lax.rsqrt(spread + EPS)


def shaped(shape, dtype=BF):
    return jax.ShapeDtypeStruct(shape, dtype)


def call(kernel, name, outs, ins, *args, flops=1):
    return pl.pallas_call(
        kernel,
        out_shape=outs,
        in_specs=ins,
        out_specs=jax.tree.map(lambda _: VMEM, outs),
        compiler_params=LIMIT,
        cost_estimate=pl.CostEstimate(flops=flops, bytes_accessed=1, transcendentals=0),
        name=name,
    )(*args)


def slots(user, position, rank):
    return (user >> 1) * 32 + (position & 3) * 8 + (user & 1) * 4 + (rank >> 2)


def column(row, start):
    piece = row[:, start : start + 128].astype(F32)
    diagonal = iota((128, 128), 0) == iota((128, 128), 1)
    return jnp.sum(jnp.where(diagonal, piece, jnp.zeros((), F32)), axis=1, keepdims=True).astype(I32)


def place_kernel(row_ref, x_ref, out_ref, ids_ref):
    row = row_ref[...]
    count = row.shape[1]
    step = 128
    zero = jnp.zeros((), F32)
    one = jnp.ones((), F32)

    def tally(mask):
        return jnp.sum(jnp.where(mask, one, zero), axis=0, keepdims=True)

    less = jnp.zeros((1, count), F32)
    ahead = jnp.zeros((1, count), F32)
    for r in range(0, count, step):
        mine = column(row, r)
        here = iota((step, count), 0) + r
        there = iota((step, count), 1)
        less = less + tally(mine < row)
        ahead = ahead + tally((mine == row) & (here < there))
    rank = ahead.astype(I32)
    slot = slots(row, less.astype(I32) + rank, rank)
    ids_ref[...] = slot
    for s in range(0, out_ref.shape[0], 256):
        table = (iota((256, count), 0) + s == slot).astype(BF)
        out_ref[s : s + 256, :] = dot(table, x_ref[...]).astype(BF)


def place(user, x):
    count, width = x.shape
    outs = (shaped((2 * count, width)), shaped((1, count), I32))
    return call(place_kernel, "place", outs, [VMEM] * 2, user.reshape(1, count), x)


def collect_kernel(ids_ref, back, out_ref):
    count = out_ref.shape[0]
    ids = ids_ref[...]
    for r in range(0, count, 256):
        mine = jnp.concatenate([column(ids, r), column(ids, r + 128)], axis=0)
        table = (iota((256, back.shape[0]), 1) == mine).astype(BF)
        out_ref[r : r + 256, :] = dot(table, back[...]).astype(BF)


def collect(ids, back):
    outs = shaped((ids.shape[1], back.shape[1]))
    return call(collect_kernel, "collect", outs, [VMEM] * 2, ids, back)


def unpack(x_ref, state_ref):
    rows, model = state_ref.shape
    width = model // TENSOR
    a, b = iota((512, 512), 0), iota((512, 512), 1)
    wanted = ((a >> 2) & 15) * 32 + (a >> 7) * 8 + ((a >> 6) & 1) * 4 + (a & 3)
    table = (wanted == b).astype(BF)
    for n in range(rows // 128):
        got = dot(table, x_ref[n * 512 : (n + 1) * 512, :]).astype(BF)
        for t in range(TENSOR):
            for u in range(USERS):
                here, there = u * (rows // USERS) + n * 64, t * 128 + u * 64
                state_ref[here : here + 64, t * width : (t + 1) * width] = got[there : there + 64]


def pack(state_ref, out_ref):
    rows, model = state_ref.shape
    width = model // TENSOR
    a, b = iota((512, 512), 0), iota((512, 512), 1)
    wanted = ((a >> 3) & 3) * 128 + ((a >> 2) & 1) * 64 + (a >> 5) * 4 + (a & 3)
    table = (wanted == b).astype(BF)
    for n in range(rows // 128):
        parts = []
        for t in range(TENSOR):
            for u in range(USERS):
                here = u * (rows // USERS) + n * 64
                parts.append(state_ref[here : here + 64, t * width : (t + 1) * width])
        out_ref[n * 512 : (n + 1) * 512, :] = dot(table, jnp.concatenate(parts, axis=0)).astype(BF)


def fetch(pairs, sems):
    copies = [
        pltpu.make_async_copy(src, dst, sems.at[i]) for i, (src, dst) in enumerate(pairs)
    ]
    for c in copies:
        c.start()
    return copies


def wait(copies):
    for c in copies:
        c.wait()


def project(state, copies, held, normed_ref, outs):
    state = state.astype(F32)
    center, scale = moments([state], state.shape[1])
    normed = ((state - center) * scale).astype(BF)
    normed_ref[...] = normed
    half = normed.shape[0] // USERS
    for k in range(TENSOR):
        copies[k].wait()
        q = silu(dot(normed, held[k])).astype(BF)
        for u in range(USERS):
            outs[u * TENSOR + k][...] = q[u * half : (u + 1) * half]


def row_call(kernel, name, outs, args, far, held, flops=1):
    return pl.pallas_call(
        kernel,
        out_shape=outs,
        in_specs=[VMEM] * len(args) + [FAR] * len(far),
        out_specs=jax.tree.map(lambda _: VMEM, outs),
        scratch_shapes=[pltpu.VMEM(h, BF) for h in held] + [pltpu.SemaphoreType.DMA((32,))],
        compiler_params=LIMIT,
        cost_estimate=pl.CostEstimate(flops=flops, bytes_accessed=1, transcendentals=0),
        name=name,
    )(*args, *far)


def row_outs(rows, width):
    full = shaped((rows, TENSOR * width))
    return (full, full) + (shaped((rows // USERS, width)),) * (USERS * TENSOR)


def blocks(refs, part, held):
    return [(ref.at[part], held.at[k]) for k, ref in enumerate(refs)]


def first(x, queries):
    count, width = x.shape
    model = TENSOR * width

    def kernel(x_ref, *refs):
        state_ref, normed_ref, *outs, held, sems = refs[TENSOR:]
        copies = fetch(blocks(refs[:TENSOR], QUERY, held), sems)
        unpack(x_ref, state_ref)
        project(state_ref[...], copies, held, normed_ref, outs)

    outs = row_outs(count // TENSOR, width)
    held = [(TENSOR, model, width)]
    state, normed, *q = row_call(kernel, "first", outs, [x], queries, held)
    return state, normed, (q[:TENSOR], q[TENSOR:])


def own(normed, q, keys, values):
    rows, model = normed.shape
    width = model // TENSOR

    def kernel(n_ref, *refs):
        q_refs, key_refs, value_refs = refs[:8], refs[8:12], refs[12:16]
        own_ref, key_held, value_held, sems = refs[16:]
        copies = fetch(blocks(key_refs, KEY, key_held) + blocks(value_refs, VALUE, value_held), sems)
        normed = n_ref[...]
        for k in range(TENSOR):
            copies[k].wait()
            key = silu(dot(normed, key_held[k])).astype(BF).astype(F32)
            copies[TENSOR + k].wait()
            value = silu(dot(normed, value_held[k])).astype(BF).astype(F32)
            query = jnp.concatenate([q_refs[u * TENSOR + k][...] for u in range(USERS)], axis=0)
            product = query.astype(F32) * key
            for h in range(0, width, DH):
                score = jnp.sum(product[:, h : h + DH], axis=1, keepdims=True)
                weight = silu(score * DH ** (-0.5))
                own_ref[:, k * width + h : k * width + h + DH] = (
                    weight * value[:, h : h + DH]
                ).astype(BF)

    held = [(TENSOR, model, width)] * 2
    return row_call(kernel, "own", shaped((rows, model)), [normed, *q[0], *q[1]], [*keys, *values], held)


def gates(normed, weights):
    rows, model = normed.shape
    width = model // TENSOR

    def kernel(n_ref, *refs):
        gate_ref, held, sems = refs[TENSOR:]
        copies = fetch(blocks(refs[:TENSOR], GATE, held), sems)
        normed = n_ref[...]
        for k in range(TENSOR):
            copies[k].wait()
            gate_ref[:, k * width : (k + 1) * width] = silu(dot(normed, held[k])).astype(BF)

    held = [(TENSOR, model, width)]
    outs = shaped((rows, model))
    return row_call(kernel, "gates", outs, [normed], weights, held, flops=8 * rows * model * model)


def attend(layer, u, lengths, q, keys, values):
    rows, width = q[0].shape
    hist = keys.shape[2]
    scale = 0.5 * DH ** (-0.5)

    def kernel(len_ref, q0, q1, q2, q3, k_ref, v_ref, *refs):
        *outs, keys_ref, values_ref, sems = refs
        first, second = fetch(
            [(k_ref.at[layer, u], keys_ref), (v_ref.at[layer, u], values_ref)], sems
        )
        first.wait()
        masked = None
        for pair in ((0, 1), (2, 3)):
            q = jnp.concatenate([(q0, q1, q2, q3)[k][...] for k in pair], axis=0)
            for h in range(0, width, DH):
                cols = slice(h, h + DH)
                s = lax.dot_general(
                    q[:, cols],
                    keys_ref[:, cols],
                    (((1,), (1,)), ((), ())),
                    preferred_element_type=F32,
                )
                s = s * scale
                w = (s * jnp.tanh(s) + s).astype(BF)
                if masked is None:
                    second.wait()
                    live = iota((hist, width), 0) < len_ref[u]
                    masked = jnp.where(live, values_ref[...], jnp.zeros((), BF))
                    values_ref[...] = masked
                got = dot(w, values_ref[:, cols]).astype(BF)
                outs[pair[0]][:, cols] = got[:rows]
                outs[pair[1]][:, cols] = got[rows:]

    return pl.pallas_call(
        kernel,
        out_shape=(shaped((rows, width)),) * TENSOR,
        in_specs=[SMEM] + [VMEM] * TENSOR + [FAR, FAR],
        out_specs=(VMEM,) * TENSOR,
        scratch_shapes=[pltpu.VMEM((hist, width), BF)] * 2 + [pltpu.SemaphoreType.DMA((2,))],
        compiler_params=LIMIT,
        cost_estimate=pl.CostEstimate(flops=1, bytes_accessed=1, transcendentals=0),
        name="attend",
    )(lengths, *q, keys, values)


def update(refs, copies, held):
    state_ref, gate_ref, own_ref = refs[:3]
    hist = refs[3:11]
    width = hist[0].shape[1]
    model = state_ref.shape[1]
    attention = []
    for k in range(TENSOR):
        got = jnp.concatenate([hist[u * TENSOR + k][...] for u in range(USERS)], axis=0)
        got = got.astype(F32) + own_ref[:, k * width : (k + 1) * width].astype(F32)
        attention.append(got.astype(BF).astype(F32))
    center, scale = moments(attention, model)
    gated = [
        ((a - center) * scale * gate_ref[:, k * width : (k + 1) * width].astype(F32)).astype(BF)
        for k, a in enumerate(attention)
    ]
    wait(copies)
    total = state_ref[...].astype(F32) + dot(jnp.concatenate(gated, axis=1), held[...])
    return total.astype(BF)


def out_rows(outs, held):
    width = outs[0].shape[0]
    return [(o, held.at[pl.ds(k * width, width)]) for k, o in enumerate(outs)]


def middle(state, gate, own_part, hist, outs, queries):
    rows, model = state.shape
    width = model // TENSOR

    def kernel(*refs):
        out_refs, query_refs = refs[11:15], refs[15:19]
        state_ref, normed_ref, *q, held_out, held, sems = refs[19:]
        copies = fetch(out_rows(out_refs, held_out) + blocks(query_refs, QUERY, held), sems)
        new = update(refs[:11], copies[:TENSOR], held_out)
        state_ref[...] = new
        project(new, copies[TENSOR:], held, normed_ref, q)

    args = [state, gate, own_part, *hist[0], *hist[1]]
    held = [(model, model), (TENSOR, model, width)]
    far = [*outs, *queries]
    state, normed, *q = row_call(kernel, "middle", row_outs(rows, width), args, far, held)
    return state, normed, (q[:TENSOR], q[TENSOR:])


def end(state, gate, own_part, hist, outs):
    rows, model = state.shape

    def kernel(*refs):
        out_ref, held, state_ref, sems = refs[15:]
        copies = fetch(out_rows(refs[11:15], held), sems)
        state_ref[...] = update(refs[:11], copies, held)
        pack(state_ref, out_ref)

    args = [state, gate, own_part, *hist[0], *hist[1]]
    out = shaped((TENSOR * rows, model // TENSOR))
    return row_call(kernel, "end", out, args, list(outs), [(model, model), state.shape])


def hop(x, k):
    return lax.ppermute(x, "tensor", [(i, i ^ k) for i in range(TENSOR)])


def wrap(x):
    total = TENSOR * lax.axis_size("cache")
    return lax.ppermute(x, ("cache", "tensor"), [(i, i ^ 6) for i in range(total)])


def spread(x, beside, across, after):
    across = tie(across, after)
    return [x, beside, across, hop(across, 1)]


def swap(blocks):
    return [blocks[0], hop(blocks[1], 1), hop(blocks[2], 2), hop(blocks[3], 3)]


def tie(x, *others):
    return lax.optimization_barrier((x,) + others)[0]


def exchange(x):
    shape = x.shape
    x = x.reshape((shape[0] // 8, 8, shape[1]))
    everyone = ("cache", "tensor")
    return lax.all_to_all(x, everyone, split_axis=0, concat_axis=0, tiled=True).reshape(shape)


def per_device(candidates, candidate_user, history_lengths, w_in, w_out, hist_keys, hist_values):
    def attention(number, u, q):
        return attend(number, u, history_lengths, q, hist_keys, hist_values)

    parts = w_in.transpose(0, 2, 1, 3)
    (gv0, qk0), (gv1, qk1) = [(parts[l, :2], parts[l, 2:]) for l in range(2)]
    far_qk0, far_gv0 = hop(qk0, 2), wrap(gv0)
    placed, ids = place(candidate_user, tie(candidates, qk0, gv0))
    rows = exchange(placed)
    beside = [hop(tie(x, placed), 1) for x in (qk0, gv0, qk1, gv1, w_out)]
    qk0 = spread(qk0, beside[0], far_qk0, placed)
    gv0 = spread(gv0, beside[1], far_gv0, placed)
    far_qk1 = wrap(tie(qk1, gv0[2]))
    rows, qk0, gv0, beside = lax.optimization_barrier((rows, qk0, gv0, beside))

    state, normed, q = first(rows, qk0)
    part = own(normed, q, qk0, gv0)
    q0, q1 = swap(q[0]), swap(q[1])
    q0, part = lax.optimization_barrier((q0, part))
    far_out0 = wrap(tie(w_out, q0[2])[0])
    far_gv1 = wrap(tie(gv1, q0[2]))
    a0 = attention(0, 0, q0)
    qk1 = spread(qk1, beside[2], far_qk1, a0[0])
    q1, _ = lax.optimization_barrier((q1, a0[0]))
    a1 = attention(0, 1, q1)
    out0 = spread(w_out[0], beside[4][0], far_out0, a1[0])
    hist = swap(a0), swap(a1)
    gate = gates(tie(normed, a1[0], *hist[0]), gv0)
    state, normed, q = middle(state, gate, part, hist, out0, qk1)

    gv1 = spread(gv1, beside[3], far_gv1, normed)
    part = own(normed, q, qk1, gv1)
    q0, q1 = swap(q[0]), swap(q[1])
    q0, part = lax.optimization_barrier((q0, part))
    far_out1 = wrap(tie(w_out, q0[2])[1])
    a0 = attention(1, 0, q0)
    q1, _ = lax.optimization_barrier((q1, a0[0]))
    a1 = attention(1, 1, q1)
    out1 = spread(w_out[1], beside[4][1], far_out1, a1[0])
    hist = swap(a0), swap(a1)
    gate = gates(tie(normed, a1[0], *hist[0]), gv1)
    out = end(state, gate, part, hist, out1)
    return collect(ids, exchange(out))


def solution(mesh):
    placed = (
        P("cache", "tensor"),
        P("cache", None),
        P("cache"),
        P(None, None, None, "tensor"),
        P(None, "tensor", None),
        P(None, "cache", None, "tensor"),
        P(None, "cache", None, "tensor"),
    )
    return jax.shard_map(
        per_device, mesh=mesh, in_specs=placed, out_specs=P("cache", "tensor"), check_vma=False
    )
```

```python
import jax
import jax.numpy as jnp
from jax import lax
from jax.experimental import pallas as pl
from jax.experimental.pallas import tpu as pltpu
from jax.sharding import PartitionSpec as P

DH = 128
EPS = 1e-05
BF = jnp.bfloat16
F32 = jnp.float32
I32 = jnp.int32
MIB = 1024 * 1024
SMEM = pl.BlockSpec(memory_space=pltpu.SMEM)
VMEM = pl.BlockSpec(memory_space=pltpu.VMEM)
FAR = pl.BlockSpec(memory_space=pltpu.HBM)
LIMIT = pltpu.CompilerParams(vmem_limit_bytes=20 * MIB)
TENSOR = 4
GATE, VALUE, QUERY, KEY = 0, 1, 0, 1
USERS = 2


def dot(a, b):
    return jnp.dot(a, b, preferred_element_type=F32)


def silu(x):
    half = 0.5 * x
    return half * jnp.tanh(half) + half


def iota(shape, axis):
    return lax.broadcasted_iota(I32, shape, axis)


def moments(parts, width):
    total = sum(jnp.sum(p, axis=1, keepdims=True) for p in parts)
    squares = sum(jnp.sum(p * p, axis=1, keepdims=True) for p in parts)
    center = total / width
    spread = squares / width - center * center
    return center, lax.rsqrt(spread + EPS)


def shaped(shape, dtype=BF):
    return jax.ShapeDtypeStruct(shape, dtype)


def call(kernel, name, outs, ins, *args, flops=1):
    return pl.pallas_call(
        kernel,
        out_shape=outs,
        in_specs=ins,
        out_specs=jax.tree.map(lambda _: VMEM, outs),
        compiler_params=LIMIT,
        cost_estimate=pl.CostEstimate(flops=flops, bytes_accessed=1, transcendentals=0),
        name=name,
    )(*args)


def slots(user, position, rank):
    return (user >> 1) * 32 + (position & 3) * 8 + (user & 1) * 4 + (rank >> 2)


def column(row, start):
    piece = row[:, start : start + 128].astype(F32)
    diagonal = iota((128, 128), 0) == iota((128, 128), 1)
    return jnp.sum(jnp.where(diagonal, piece, jnp.zeros((), F32)), axis=1, keepdims=True).astype(I32)


def place_kernel(row_ref, x_ref, out_ref, ids_ref):
    row = row_ref[...]
    count = row.shape[1]
    step = 128
    zero = jnp.zeros((), F32)
    one = jnp.ones((), F32)

    def tally(mask):
        return jnp.sum(jnp.where(mask, one, zero), axis=0, keepdims=True)

    less = jnp.zeros((1, count), F32)
    ahead = jnp.zeros((1, count), F32)
    for r in range(0, count, step):
        mine = column(row, r)
        here = iota((step, count), 0) + r
        there = iota((step, count), 1)
        less = less + tally(mine < row)
        ahead = ahead + tally((mine == row) & (here < there))
    rank = ahead.astype(I32)
    slot = slots(row, less.astype(I32) + rank, rank)
    ids_ref[...] = slot
    for s in range(0, out_ref.shape[0], 256):
        table = (iota((256, count), 0) + s == slot).astype(BF)
        out_ref[s : s + 256, :] = dot(table, x_ref[...]).astype(BF)


def place(user, x):
    count, width = x.shape
    outs = (shaped((2 * count, width)), shaped((1, count), I32))
    return call(place_kernel, "place", outs, [VMEM] * 2, user.reshape(1, count), x)


def collect_kernel(ids_ref, back, out_ref):
    count = out_ref.shape[0]
    ids = ids_ref[...]
    for r in range(0, count, 256):
        mine = jnp.concatenate([column(ids, r), column(ids, r + 128)], axis=0)
        table = (iota((256, back.shape[0]), 1) == mine).astype(BF)
        out_ref[r : r + 256, :] = dot(table, back[...]).astype(BF)


def collect(ids, back):
    outs = shaped((ids.shape[1], back.shape[1]))
    return call(collect_kernel, "collect", outs, [VMEM] * 2, ids, back)


def unpack(x_ref, state_ref):
    rows, model = state_ref.shape
    width = model // TENSOR
    a, b = iota((512, 512), 0), iota((512, 512), 1)
    wanted = ((a >> 2) & 15) * 32 + (a >> 7) * 8 + ((a >> 6) & 1) * 4 + (a & 3)
    table = (wanted == b).astype(BF)
    for n in range(rows // 128):
        got = dot(table, x_ref[n * 512 : (n + 1) * 512, :]).astype(BF)
        for t in range(TENSOR):
            for u in range(USERS):
                here, there = u * (rows // USERS) + n * 64, t * 128 + u * 64
                state_ref[here : here + 64, t * width : (t + 1) * width] = got[there : there + 64]


def pack(state_ref, out_ref):
    rows, model = state_ref.shape
    width = model // TENSOR
    a, b = iota((512, 512), 0), iota((512, 512), 1)
    wanted = ((a >> 3) & 3) * 128 + ((a >> 2) & 1) * 64 + (a >> 5) * 4 + (a & 3)
    table = (wanted == b).astype(BF)
    for n in range(rows // 128):
        parts = []
        for t in range(TENSOR):
            for u in range(USERS):
                here = u * (rows // USERS) + n * 64
                parts.append(state_ref[here : here + 64, t * width : (t + 1) * width])
        out_ref[n * 512 : (n + 1) * 512, :] = dot(table, jnp.concatenate(parts, axis=0)).astype(BF)


def fetch(pairs, sems):
    copies = [
        pltpu.make_async_copy(src, dst, sems.at[i]) for i, (src, dst) in enumerate(pairs)
    ]
    for c in copies:
        c.start()
    return copies


def wait(copies):
    for c in copies:
        c.wait()


def project(state, copies, held, normed_ref, outs):
    state = state.astype(F32)
    center, scale = moments([state], state.shape[1])
    normed = ((state - center) * scale).astype(BF)
    normed_ref[...] = normed
    half = normed.shape[0] // USERS
    for k in range(TENSOR):
        copies[k].wait()
        q = silu(dot(normed, held[k])).astype(BF)
        for u in range(USERS):
            outs[u * TENSOR + k][...] = q[u * half : (u + 1) * half]


def row_call(kernel, name, outs, args, far, held, flops=1):
    return pl.pallas_call(
        kernel,
        out_shape=outs,
        in_specs=[VMEM] * len(args) + [FAR] * len(far),
        out_specs=jax.tree.map(lambda _: VMEM, outs),
        scratch_shapes=[pltpu.VMEM(h, BF) for h in held] + [pltpu.SemaphoreType.DMA((32,))],
        compiler_params=LIMIT,
        cost_estimate=pl.CostEstimate(flops=flops, bytes_accessed=1, transcendentals=0),
        name=name,
    )(*args, *far)


def row_outs(rows, width):
    full = shaped((rows, TENSOR * width))
    return (full, full) + (shaped((rows // USERS, width)),) * (USERS * TENSOR)


def blocks(refs, part, held):
    return [(ref.at[part], held.at[k]) for k, ref in enumerate(refs)]


def first(x, queries):
    count, width = x.shape
    model = TENSOR * width

    def kernel(x_ref, *refs):
        state_ref, normed_ref, *outs, held, sems = refs[TENSOR:]
        copies = fetch(blocks(refs[:TENSOR], QUERY, held), sems)
        unpack(x_ref, state_ref)
        project(state_ref[...], copies, held, normed_ref, outs)

    outs = row_outs(count // TENSOR, width)
    held = [(TENSOR, model, width)]
    state, normed, *q = row_call(kernel, "first", outs, [x], queries, held)
    return state, normed, (q[:TENSOR], q[TENSOR:])


def own(normed, q, keys, values):
    rows, model = normed.shape
    width = model // TENSOR

    def kernel(n_ref, *refs):
        q_refs, key_refs, value_refs = refs[:8], refs[8:12], refs[12:16]
        own_ref, key_held, value_held, sems = refs[16:]
        copies = fetch(blocks(key_refs, KEY, key_held) + blocks(value_refs, VALUE, value_held), sems)
        normed = n_ref[...]
        for k in range(TENSOR):
            copies[k].wait()
            key = silu(dot(normed, key_held[k])).astype(BF).astype(F32)
            copies[TENSOR + k].wait()
            value = silu(dot(normed, value_held[k])).astype(BF).astype(F32)
            query = jnp.concatenate([q_refs[u * TENSOR + k][...] for u in range(USERS)], axis=0)
            product = query.astype(F32) * key
            for h in range(0, width, DH):
                score = jnp.sum(product[:, h : h + DH], axis=1, keepdims=True)
                weight = silu(score * DH ** (-0.5))
                own_ref[:, k * width + h : k * width + h + DH] = (
                    weight * value[:, h : h + DH]
                ).astype(BF)

    held = [(TENSOR, model, width)] * 2
    return row_call(kernel, "own", shaped((rows, model)), [normed, *q[0], *q[1]], [*keys, *values], held)


def gates(normed, weights):
    rows, model = normed.shape
    width = model // TENSOR

    def kernel(n_ref, *refs):
        gate_ref, held, sems = refs[TENSOR:]
        copies = fetch(blocks(refs[:TENSOR], GATE, held), sems)
        normed = n_ref[...]
        for k in range(TENSOR):
            copies[k].wait()
            gate_ref[:, k * width : (k + 1) * width] = silu(dot(normed, held[k])).astype(BF)

    held = [(TENSOR, model, width)]
    outs = shaped((rows, model))
    return row_call(kernel, "gates", outs, [normed], weights, held, flops=8 * rows * model * model)


def attend(layer, u, lengths, q, keys, values):
    rows, width = q[0].shape
    hist = keys.shape[2]
    scale = 0.5 * DH ** (-0.5)

    def kernel(len_ref, q0, q1, q2, q3, k_ref, v_ref, *refs):
        *outs, values_ref = refs
        live = iota((hist, width), 0) < len_ref[u]
        values_ref[...] = jnp.where(live, v_ref[layer, u], jnp.zeros((), BF))
        for pair in ((0, 1), (2, 3)):
            q = jnp.concatenate([(q0, q1, q2, q3)[k][...] for k in pair], axis=0)
            for h in range(0, width, DH):
                cols = slice(h, h + DH)
                s = lax.dot_general(
                    q[:, cols],
                    k_ref[layer, u, :, cols],
                    (((1,), (1,)), ((), ())),
                    preferred_element_type=F32,
                )
                s = s * scale
                w = (s * jnp.tanh(s) + s).astype(BF)
                got = dot(w, values_ref[:, cols]).astype(BF)
                outs[pair[0]][:, cols] = got[:rows]
                outs[pair[1]][:, cols] = got[rows:]

    return pl.pallas_call(
        kernel,
        out_shape=(shaped((rows, width)),) * TENSOR,
        in_specs=[SMEM] + [VMEM] * (TENSOR + 2),
        out_specs=(VMEM,) * TENSOR,
        scratch_shapes=[pltpu.VMEM((hist, width), BF)],
        compiler_params=LIMIT,
        cost_estimate=pl.CostEstimate(flops=1, bytes_accessed=1, transcendentals=0),
        name="attend",
    )(lengths, *q, keys, values)


def update(refs, copies, held):
    state_ref, gate_ref, own_ref = refs[:3]
    hist = refs[3:11]
    width = hist[0].shape[1]
    model = state_ref.shape[1]
    attention = []
    for k in range(TENSOR):
        got = jnp.concatenate([hist[u * TENSOR + k][...] for u in range(USERS)], axis=0)
        got = got.astype(F32) + own_ref[:, k * width : (k + 1) * width].astype(F32)
        attention.append(got.astype(BF).astype(F32))
    center, scale = moments(attention, model)
    gated = [
        ((a - center) * scale * gate_ref[:, k * width : (k + 1) * width].astype(F32)).astype(BF)
        for k, a in enumerate(attention)
    ]
    wait(copies)
    total = state_ref[...].astype(F32) + dot(jnp.concatenate(gated, axis=1), held[...])
    return total.astype(BF)


def out_rows(outs, held):
    width = outs[0].shape[0]
    return [(o, held.at[pl.ds(k * width, width)]) for k, o in enumerate(outs)]


def middle(state, gate, own_part, hist, outs, queries):
    rows, model = state.shape
    width = model // TENSOR

    def kernel(*refs):
        out_refs, query_refs = refs[11:15], refs[15:19]
        state_ref, normed_ref, *q, held_out, held, sems = refs[19:]
        copies = fetch(out_rows(out_refs, held_out) + blocks(query_refs, QUERY, held), sems)
        new = update(refs[:11], copies[:TENSOR], held_out)
        state_ref[...] = new
        project(new, copies[TENSOR:], held, normed_ref, q)

    args = [state, gate, own_part, *hist[0], *hist[1]]
    held = [(model, model), (TENSOR, model, width)]
    far = [*outs, *queries]
    state, normed, *q = row_call(kernel, "middle", row_outs(rows, width), args, far, held)
    return state, normed, (q[:TENSOR], q[TENSOR:])


def end(state, gate, own_part, hist, outs):
    rows, model = state.shape

    def kernel(*refs):
        out_ref, held, state_ref, sems = refs[15:]
        copies = fetch(out_rows(refs[11:15], held), sems)
        state_ref[...] = update(refs[:11], copies, held)
        pack(state_ref, out_ref)

    args = [state, gate, own_part, *hist[0], *hist[1]]
    out = shaped((TENSOR * rows, model // TENSOR))
    return row_call(kernel, "end", out, args, list(outs), [(model, model), state.shape])


def hop(x, k):
    return lax.ppermute(x, "tensor", [(i, i ^ k) for i in range(TENSOR)])


def wrap(x):
    total = TENSOR * lax.axis_size("cache")
    return lax.ppermute(x, ("cache", "tensor"), [(i, i ^ 6) for i in range(total)])


def spread(x, beside, across, after):
    across = tie(across, after)
    return [x, beside, across, hop(across, 1)]


def swap(blocks):
    return [blocks[0], hop(blocks[1], 1), hop(blocks[2], 2), hop(blocks[3], 3)]


def tie(x, *others):
    return lax.optimization_barrier((x,) + others)[0]


def exchange(x):
    shape = x.shape
    x = x.reshape((shape[0] // 8, 8, shape[1]))
    everyone = ("cache", "tensor")
    return lax.all_to_all(x, everyone, split_axis=0, concat_axis=0, tiled=True).reshape(shape)


def per_device(candidates, candidate_user, history_lengths, w_in, w_out, hist_keys, hist_values):
    def attention(number, u, q):
        return attend(number, u, history_lengths, q, hist_keys, hist_values)

    parts = w_in.transpose(0, 2, 1, 3)
    (gv0, qk0), (gv1, qk1) = [(parts[l, :2], parts[l, 2:]) for l in range(2)]
    far_qk0, far_gv0 = hop(qk0, 2), wrap(gv0)
    placed, ids = place(candidate_user, tie(candidates, qk0, gv0))
    rows = exchange(placed)
    beside = [hop(tie(x, placed), 1) for x in (qk0, gv0, qk1, gv1, w_out)]
    qk0 = spread(qk0, beside[0], far_qk0, placed)
    gv0 = spread(gv0, beside[1], far_gv0, placed)
    far_qk1 = wrap(tie(qk1, gv0[2]))
    rows, qk0, gv0, beside = lax.optimization_barrier((rows, qk0, gv0, beside))

    state, normed, q = first(rows, qk0)
    part = own(normed, q, qk0, gv0)
    q0, q1 = swap(q[0]), swap(q[1])
    q0, part = lax.optimization_barrier((q0, part))
    far_out0 = wrap(tie(w_out, q0[2])[0])
    far_gv1 = wrap(tie(gv1, q0[2]))
    a0 = attention(0, 0, q0)
    qk1 = spread(qk1, beside[2], far_qk1, a0[0])
    q1, _ = lax.optimization_barrier((q1, a0[0]))
    a1 = attention(0, 1, q1)
    out0 = spread(w_out[0], beside[4][0], far_out0, a1[0])
    hist = swap(a0), swap(a1)
    gate = gates(tie(normed, a1[0], *hist[0]), gv0)
    state, normed, q = middle(state, gate, part, hist, out0, qk1)

    gv1 = spread(gv1, beside[3], far_gv1, normed)
    part = own(normed, q, qk1, gv1)
    q0, q1 = swap(q[0]), swap(q[1])
    q0, part = lax.optimization_barrier((q0, part))
    far_out1 = wrap(tie(w_out, q0[2])[1])
    a0 = attention(1, 0, q0)
    q1, _ = lax.optimization_barrier((q1, a0[0]))
    a1 = attention(1, 1, q1)
    out1 = spread(w_out[1], beside[4][1], far_out1, a1[0])
    hist = swap(a0), swap(a1)
    gate = gates(tie(normed, a1[0], *hist[0]), gv1)
    out = end(state, gate, part, hist, out1)
    return collect(ids, exchange(out))


def solution(mesh):
    placed = (
        P("cache", "tensor"),
        P("cache", None),
        P("cache"),
        P(None, None, None, "tensor"),
        P(None, "tensor", None),
        P(None, "cache", None, "tensor"),
        P(None, "cache", None, "tensor"),
    )
    return jax.shard_map(
        per_device, mesh=mesh, in_specs=placed, out_specs=P("cache", "tensor"), check_vma=False
    )
```
